256 devices in a mesh: prow: 8 (over y, core), pcol: 32 (over x, z).
Axes of the slice: x: 4, y: 4, z: 8, core: 2. Of those that a mesh axis runs over, the one named last changes fastest.
Arguments:
- covariance: bfloat16 [8, 8, 256, 2, 32, 256], P(None, 'prow', None, None, 'pcol'), may hold values from 0 to 3, as said below
Outputs:
- factored: float32 [8, 8, 256, 2, 32, 256], P(None, 'prow', None, None, 'pcol')
The draws below stay inside these ranges and needn't reach their ends.
Inputs may be any that keep to these rules, and one draw needn't show every extreme that they name: `covariance`: the matrix is symmetric and positive definite.
All inputs are finite; a program needn't handle non-finite values.
Results may differ from the reference program's by a relative error of at most 0.0003.
Values sent between devices are 32-bit elements; how exact they have to be, the bound alone decides.
A program may use at most 64 MiB of HBM per device.

```python
from functools import partial
import jax
import jax.numpy as jnp
from jax import lax

N = 16384
B = 256
PANELS = 4
GRID = 128
RT = 8
CT = 2
N_PROW = 8
N_PCOL = 32


matern_slope = 0.14433756729740643


def matern_rows(coords, nugget, tile_index):
    start = tile_index * B
    own_xy = lax.dynamic_slice_in_dim(coords, start, B, 1)
    x_diff = own_xy[0][:, None] - coords[0][None, :]
    y_diff = own_xy[1][:, None] - coords[1][None, :]
    distance = jnp.sqrt(x_diff * x_diff + y_diff * y_diff)
    scaled = matern_slope * distance
    values = (1.0 + scaled) * jnp.exp(-scaled)
    row_ids = start + jnp.arange(B, dtype=jnp.int32)
    col_ids = jnp.arange(N, dtype=jnp.int32)
    own_nugget = lax.dynamic_slice_in_dim(nugget, start, B, 0)
    values = values + jnp.where(row_ids[:, None] == col_ids[None, :], own_nugget[:, None], 0.0)
    return values.astype(jnp.bfloat16)


def draw_covariance(key, part):
    key = jax.random.fold_in(key, 11)
    place_key, nugget_key = jax.random.split(key)
    coords = jax.random.randint(place_key, (2, N), 0, GRID).astype(jnp.float32)
    nugget = jnp.exp(jax.random.uniform(nugget_key, (N,), jnp.float32, math_low, math_high))
    rows = lax.map(partial(matern_rows, coords, nugget), jnp.arange(N // B, dtype=jnp.int32))
    return rows.reshape(RT, N_PROW, B, CT, N_PCOL, B)


math_low = -0.6931471805599453


math_high = 0.6931471805599453


def setup_inputs(seed: int = 0) -> dict:
    keys = jax.random.split(jax.random.key(seed), 2)
    covariance = draw_covariance(jax.random.fold_in(keys[1], 71), 0)
    return {"covariance": covariance}


def reference(covariance):
    matrix = covariance.astype(jnp.float32).reshape(N, N)
    identity = jnp.eye(B, dtype=jnp.float32)
    columns = []
    for panel_index in range(PANELS):
        lkk = jnp.linalg.cholesky(matrix[:B, :B])
        linv = lax.linalg.triangular_solve(lkk, identity, left_side=True, lower=True)
        below = jnp.dot(matrix[B:, :B].astype(jnp.float32), linv.T.astype(jnp.float32), precision=lax.Precision.HIGHEST, preferred_element_type=jnp.float32)
        upper_zero = jnp.zeros((panel_index * B, B), jnp.float32)
        columns.append(jnp.concatenate([upper_zero, lkk, below], axis=0))
        matrix = matrix[B:, B:] - jnp.dot(below.astype(jnp.float32), below.T.astype(jnp.float32), precision=lax.Precision.HIGHEST, preferred_element_type=jnp.float32)
    done = PANELS * B
    left_part = jnp.concatenate(columns, axis=1)
    right_part = jnp.concatenate([jnp.zeros((done, N - done), jnp.float32), matrix], axis=0)
    factored = jnp.concatenate([left_part, right_part], axis=1)
    return factored.reshape(N // B // N_PROW, N_PROW, B, N // B // N_PCOL, N_PCOL, B)
```

```python
import functools
import jax
import jax.numpy as jnp
from jax import lax
from jax.experimental import pallas as pl
from jax.experimental.pallas import tpu as pltpu
from jax.sharding import PartitionSpec as P

B = 256
NP = 4
TOP = NP * B
F32 = jnp.float32
BF16 = jnp.bfloat16
MESH = pl.DeviceIdType.MESH


def split(a):
    hi = a.astype(BF16)
    return hi, (a - hi.astype(F32)).astype(BF16)


def dot1(a, b):
    return jnp.dot(a, b, preferred_element_type=F32)


def dot3(a, b):
    ah, al = split(a)
    bh, bl = split(b)
    return dot1(ah, bh) + (dot1(ah, bl) + dot1(al, bh))


def spread_kernel(a_ref, m_ref, g_ref, rg, rm, so, sf, st):
    p = lax.axis_index("prow")
    q = lax.axis_index("pcol")
    x = q // 8
    z = q % 8
    par = p % 2
    sib = p + 1 - 2 * par

    barrier = pltpu.get_barrier_semaphore()
    partners = [(lax.rem(p + d, 8), q) for d in range(1, 8)]
    partners += [(p, lax.rem(q + 8 * d, 32)) for d in (1, 2, 3)]
    partners += [(p, 8 * x + lax.rem(z + d, 8)) for d in (1, 7)]
    for pp, qq in partners:
        pl.semaphore_signal(barrier, inc=1, device_id=(pp, qq), device_id_type=MESH)
    pl.semaphore_wait(barrier, len(partners))

    def send(src, dst, ssem, rsem, pp, qq):
        return pltpu.make_async_remote_copy(
            src_ref=src, dst_ref=dst, send_sem=ssem, recv_sem=rsem,
            device_id=(pp, qq), device_id_type=MESH,
        )

    def gslot(k, c):
        return g_ref.at[pl.ds(pl.multiple_of(k * B, B), B), pl.ds(c * B, B)]

    def mslot(k, kc):
        return m_ref.at[pl.ds(pl.multiple_of(k * B, B), B), pl.ds(kc * B, B)]

    def origin(c):
        for n, d in enumerate((2, 6, 4, None)):
            pp = sib if d is None else lax.rem(p + d, 8)
            yield send(a_ref.at[c], gslot(p, c), so.at[c, n], rg.at[p, c], pp, q)

    def relay(k, c):
        return send(gslot(k, c), gslot(k, c), sf.at[k, c], rg.at[k, c], sib, q)

    def strips(c):
        @pl.when(p < NP)
        def _():
            for cp in origin(c):
                cp.start()
            g_ref[pl.ds(pl.multiple_of(p * B, B), B), c * B:(c + 1) * B] = a_ref[c]
        for i in range(2):
            k = par + 2 * i

            @pl.when(k != p)
            def _():
                relay(k, c).wait_recv()
                relay(k, c).start()

    def tile_sends(i, kc):
        k = par + 2 * i
        d = lax.rem(z + 8 - kc, 8)
        slot = mslot(k, kc)
        rsem = rm.at[k, kc]
        out = []
        for n in range(3):
            out.append(((d == 0) & (x == 0),
                        send(slot, slot, st.at[i, kc, n], rsem, p, lax.rem(q + 8 * (n + 1), 32))))
        out.append((d < 4, send(slot, slot, st.at[i, kc, 3], rsem, p, 8 * x + lax.rem(z + 1, 8))))
        out.append(((d == 0) | (d > 5), send(slot, slot, st.at[i, kc, 4], rsem, p, 8 * x + lax.rem(z + 7, 8))))
        out.append((None, send(slot, slot, st.at[i, kc, 5], rsem, sib, q)))
        return d, out

    strips(0)
    for i in range(2):
        for kc in range(NP):
            k = par + 2 * i

            @pl.when(k <= kc)
            def _():
                d, sends = tile_sends(i, kc)
                here = (d == 0) & (x == 0)

                @pl.when(here)
                def _():
                    rows = pl.ds(pl.multiple_of(k * B, B), B)
                    m_ref[rows, kc * B:(kc + 1) * B] = g_ref[rows, 0:B]

                @pl.when(jnp.logical_not(here))
                def _():
                    sends[5][1].wait_recv()
                for cond, cp in sends:
                    if cond is None:
                        cp.start()
                    else:
                        pl.when(cond)(cp.start)
    strips(1)

    for i in range(2):
        k = 1 - par + 2 * i
        for c in range(2):
            relay(k, c).wait_recv()
        for kc in range(NP):
            @pl.when(k <= kc)
            def _():
                slot = mslot(k, kc)
                send(slot, slot, st.at[i, kc, 5], rm.at[k, kc], sib, q).wait_recv()

    for c in range(2):
        @pl.when(p < NP)
        def _():
            for cp in origin(c):
                cp.wait_send()
        for i in range(2):
            k = par + 2 * i

            @pl.when(k != p)
            def _():
                relay(k, c).wait_send()
    for i in range(2):
        for kc in range(NP):
            @pl.when(par + 2 * i <= kc)
            def _():
                for cond, cp in tile_sends(i, kc)[1]:
                    if cond is None:
                        cp.wait_send()
                    else:
                        pl.when(cond)(cp.wait_send)


def spread(a):
    dma = pltpu.SemaphoreType.DMA
    return pl.pallas_call(
        spread_kernel,
        out_shape=(jax.ShapeDtypeStruct((TOP, TOP), F32), jax.ShapeDtypeStruct((TOP, 2 * B), F32)),
        in_specs=[pl.BlockSpec(memory_space=pltpu.VMEM)],
        out_specs=[pl.BlockSpec(memory_space=pltpu.VMEM)] * 2,
        scratch_shapes=[dma((NP, 2)), dma((NP, NP)), dma((2, 4)), dma((NP, 2)), dma((2, NP, 6))],
        compiler_params=pltpu.CompilerParams(
            collective_id=1, has_side_effects=True, vmem_limit_bytes=32 * 1024 * 1024),
        name="spread",
    )(a)


def panel(R, j, sub, lane):
    for g in range(4):
        c0 = j + 8 * g
        lt = c0 // 128
        o = c0 % 128
        cb = {}
        for h in range(g, 4):
            for t in range(8):
                cb[h, t] = jnp.broadcast_to(R[h][lt][:, o + t:o + t + 1], (8, 128))
        inblk = (lane >= o) & (lane < o + 8)
        R[g][lt] = jnp.where(inblk, jnp.where(lane - o == sub, 1.0, 0.0), R[g][lt])
        for h in range(g + 1, 4):
            R[h][lt] = jnp.where(inblk, 0.0, R[h][lt])
        scale = jnp.zeros((8, 128), F32)
        for t in range(8):
            piv = jnp.broadcast_to(cb[g, t][t:t + 1, :], (8, 128))
            inv = 1.0 / piv
            scale = jnp.where(sub == t, lax.rsqrt(piv), scale)
            rows = [jnp.broadcast_to(R[g][l][t:t + 1, :], (8, 128)) for l in range(2)]
            crow = {u: jnp.broadcast_to(cb[g, u][t:t + 1, :], (8, 128)) for u in range(t + 1, 8)}
            for h in range(g, 4):
                f = cb[h, t] * inv
                if h == g:
                    f = jnp.where(sub > t, f, 0.0)
                for l in range(2):
                    R[h][l] = R[h][l] - f * rows[l]
                for u in range(t + 1, 8):
                    cb[h, u] = cb[h, u] - f * crow[u]
        for u in range(1, 8):
            R[g][lt] = jnp.where((lane == o + u) & (sub < u), cb[g, u], R[g][lt])
        for l in range(2):
            R[g][l] = R[g][l] * scale
    return R


def factor_tile(T):
    sub = lax.broadcasted_iota(jnp.int32, (8, 128), 0)
    lane = lax.broadcasted_iota(jnp.int32, (8, 128), 1)
    pr = lax.broadcasted_iota(jnp.int32, (32, B), 0)
    pc = lax.broadcasted_iota(jnp.int32, (32, B), 1)
    for jb in range(8):
        j = 32 * jb
        R = [[T[j + 8 * g:j + 8 * g + 8, 128 * l:128 * l + 128] for l in range(2)] for g in range(4)]
        R = panel(R, j, sub, lane)
        rows = jnp.concatenate([jnp.concatenate(r, axis=1) for r in R], axis=0)
        T[j:j + 32, :] = rows
        if jb < 7:
            left = rows.T[j + 32:, :]
            n = B - j - 32
            ln = lax.broadcasted_iota(jnp.int32, (n, B), 1)
            low = jnp.where((ln >= j) & (ln < j + 32), 0.0, T[j + 32:, :])
            rows = jnp.where((pc < j + 32) & (pc > j + pr), 0.0, rows)
            T[j + 32:, :] = low - dot3(left, rows)


def factor_kernel(m_ref, g_ref, whi_ref, wlo_ref, l_ref, S, T, W):
    p = lax.axis_index("prow")
    q = lax.axis_index("pcol")
    S[:, 0:TOP] = m_ref[...]
    S[:, TOP:TOP + 2 * B] = g_ref[...]
    row = lax.broadcasted_iota(jnp.int32, (B, B), 0)
    col = lax.broadcasted_iota(jnp.int32, (B, B), 1)

    def tile(i):
        return pl.ds(pl.multiple_of(i * B, B), B)

    def step(k, _):
        T[...] = S[tile(k), tile(k)]
        factor_tile(T)
        S[tile(k), tile(k)] = T[...]
        X = jnp.where(row >= col, T[...], 0.0)

        def solve(m, _):
            S[tile(k), tile(m)] = dot3(X, S[tile(k), tile(m)])
            return 0

        lax.fori_loop(k + 1, NP + 2, solve, 0)

        def trail(i, _):
            left = S[tile(k), tile(i)].T

            def inner(m, _):
                S[tile(i), tile(m)] = S[tile(i), tile(m)] - dot3(left, S[tile(k), tile(m)])
                return 0

            lax.fori_loop(i, NP + 2, inner, 0)
            return 0

        lax.fori_loop(k + 1, NP, trail, 0)
        return 0

    lax.fori_loop(0, NP, step, 0)

    kq = jnp.minimum(q, NP - 1)
    kp = jnp.minimum(p, NP - 1)
    u = S[tile(kq), tile(kp)]
    u_diag = jnp.where(col > row, u, jnp.where(col == row, 1.0 / u, 0.0))
    u = jnp.where(kp == kq, u_diag, jnp.where(kq < kp, u, 0.0))
    l_ref[...] = u.T

    col2 = lax.broadcasted_iota(jnp.int32, (B, 2 * B), 1)
    row2 = lax.broadcasted_iota(jnp.int32, (B, 2 * B), 0)
    for k in (3, 2, 1, 0):
        unit = jnp.where((row2 == col2) & (q == k), 1.0, 0.0)
        acc = jnp.where((col2 < B) & (q < NP), unit, S[k * B:(k + 1) * B, TOP:TOP + 2 * B])
        for m in range(k + 1, NP):
            acc = acc - dot3(S[k * B:(k + 1) * B, m * B:(m + 1) * B], W[m * B:(m + 1) * B, :])
        X = jnp.where(row >= col, S[k * B:(k + 1) * B, k * B:(k + 1) * B], 0.0)
        w = dot3(X.T, acc)
        W[k * B:(k + 1) * B, :] = w
        hi, lo = split(w)
        whi_ref[k * B:(k + 1) * B, :] = hi
        wlo_ref[k * B:(k + 1) * B, :] = lo


def factor(m11, g):
    vmem = pl.BlockSpec(memory_space=pltpu.VMEM)
    return pl.pallas_call(
        factor_kernel,
        out_shape=(
            jax.ShapeDtypeStruct((TOP, 2 * B), BF16),
            jax.ShapeDtypeStruct((TOP, 2 * B), BF16),
            jax.ShapeDtypeStruct((B, B), F32),
        ),
        in_specs=[vmem, vmem],
        out_specs=[vmem, vmem, vmem],
        scratch_shapes=[
            pltpu.VMEM((TOP, TOP + 2 * B), F32),
            pltpu.VMEM((B, B), F32),
            pltpu.VMEM((TOP, 2 * B), F32),
        ],
        compiler_params=pltpu.CompilerParams(vmem_limit_bytes=40 * 1024 * 1024),
        cost_estimate=pl.CostEstimate(
            flops=60_000_000_000, bytes_accessed=8_000_000, transcendentals=0),
        name="factor",
    )(m11, g)


def update_kernel(b_ref, m_ref, whi_ref, wlo_ref, l_ref, o_ref):
    r = pl.program_id(0)
    p = lax.axis_index("prow")
    q = lax.axis_index("pcol")
    acc = jnp.zeros((B, 2 * B), F32)
    for k in range(NP):
        left = b_ref[k].astype(BF16)
        acc = acc + dot1(left, whi_ref[k * B:(k + 1) * B, :])
        acc = acc + dot1(left, wlo_ref[k * B:(k + 1) * B, :])
    m = m_ref[0].astype(F32)
    top = (r == 0) & (p < NP)
    factor_col = q < NP
    c0 = jnp.where(factor_col, acc[:, 0:B], m[:, 0:B] - acc[:, 0:B])
    c0 = jnp.where(top, jnp.where(factor_col, l_ref[...], 0.0), c0)
    c1 = jnp.where(top, 0.0, m[:, B:] - acc[:, B:])
    for n, part in enumerate((c0[:, :128], c0[:, 128:], c1[:, :128], c1[:, 128:])):
        o_ref[pl.ds(n, B, stride=4), :] = part


def update(bulk, mine, whi, wlo, ltile):
    return pl.pallas_call(
        update_kernel,
        grid=(8,),
        out_shape=jax.ShapeDtypeStruct((8 * 4 * B, 128), F32),
        in_specs=[
            pl.BlockSpec((4, B, B), lambda r: (2 * (r % 4) + r // 4, 0, 0)),
            pl.BlockSpec((1, B, 2 * B), lambda r: (r, 0, 0)),
            pl.BlockSpec((TOP, 2 * B), lambda r: (0, 0)),
            pl.BlockSpec((TOP, 2 * B), lambda r: (0, 0)),
            pl.BlockSpec((B, B), lambda r: (0, 0)),
        ],
        out_specs=pl.BlockSpec((4 * B, 128), lambda r: (r, 0)),
        compiler_params=pltpu.CompilerParams(vmem_limit_bytes=32 * 1024 * 1024),
        cost_estimate=pl.CostEstimate(
            flops=4_300_000_000, bytes_accessed=16_000_000, transcendentals=0),
        name="update",
    )(bulk, mine, whi, wlo, ltile)


def local(covariance):
    mine = covariance.reshape(8, B, 2, B)
    strip = mine[0].astype(F32)
    a = strip.transpose(1, 0, 2)
    at = strip.transpose(1, 2, 0)
    mine = mine.reshape(8, B, 2 * B)
    tile = jnp.zeros((B, B), F32)
    for c in range(2):
        perm = [
            (k * 32 + 8 * x + z, z * 32 + 8 * x + 4 * c + k)
            for k in range(NP) for x in range(4) for z in range(8)
        ]
        tile = tile + lax.ppermute(at[c], ("prow", "pcol"), perm)
    bulk = lax.all_gather(tile, "pcol")
    m11, g = spread(a)
    whi, wlo, ltile = factor(m11, g)
    out = update(bulk, mine, whi, wlo, ltile)
    return out.reshape(8, 1, B, 2, 1, B)


def solution(mesh):
    in_specs = (P(None, "prow", None, None, "pcol", None),)
    out_specs = P(None, "prow", None, None, "pcol", None)
    return jax.shard_map(local, mesh=mesh, in_specs=in_specs, out_specs=out_specs, check_vma=False)
```

```python
import functools
import jax
import jax.numpy as jnp
from jax import lax
from jax.experimental import pallas as pl
from jax.experimental.pallas import tpu as pltpu
from jax.sharding import PartitionSpec as P

B = 256
NP = 4
TOP = NP * B
F32 = jnp.float32
BF16 = jnp.bfloat16
MESH = pl.DeviceIdType.MESH


def split(a):
    hi = a.astype(BF16)
    return hi, (a - hi.astype(F32)).astype(BF16)


def dot1(a, b):
    return jnp.dot(a, b, preferred_element_type=F32)


def dot3(a, b):
    ah, al = split(a)
    bh, bl = split(b)
    return dot1(ah, bh) + (dot1(ah, bl) + dot1(al, bh))


def panel(R, j, sub, lane):
    for g in range(4):
        c0 = j + 8 * g
        lt = c0 // 128
        o = c0 % 128
        cb = {}
        for h in range(g, 4):
            for t in range(8):
                cb[h, t] = jnp.broadcast_to(R[h][lt][:, o + t:o + t + 1], (8, 128))
        inblk = (lane >= o) & (lane < o + 8)
        R[g][lt] = jnp.where(inblk, jnp.where(lane - o == sub, 1.0, 0.0), R[g][lt])
        for h in range(g + 1, 4):
            R[h][lt] = jnp.where(inblk, 0.0, R[h][lt])
        scale = jnp.zeros((8, 128), F32)
        for t in range(8):
            piv = jnp.broadcast_to(cb[g, t][t:t + 1, :], (8, 128))
            inv = 1.0 / piv
            scale = jnp.where(sub == t, lax.rsqrt(piv), scale)
            rows = [jnp.broadcast_to(R[g][l][t:t + 1, :], (8, 128)) for l in range(2)]
            crow = {u: jnp.broadcast_to(cb[g, u][t:t + 1, :], (8, 128)) for u in range(t + 1, 8)}
            for h in range(g, 4):
                f = cb[h, t] * inv
                if h == g:
                    f = jnp.where(sub > t, f, 0.0)
                for l in range(2):
                    R[h][l] = R[h][l] - f * rows[l]
                for u in range(t + 1, 8):
                    cb[h, u] = cb[h, u] - f * crow[u]
        for u in range(1, 8):
            R[g][lt] = jnp.where((lane == o + u) & (sub < u), cb[g, u], R[g][lt])
        for l in range(2):
            R[g][l] = R[g][l] * scale
    return R


def factor_tile(T, between):
    sub = lax.broadcasted_iota(jnp.int32, (8, 128), 0)
    lane = lax.broadcasted_iota(jnp.int32, (8, 128), 1)
    pr = lax.broadcasted_iota(jnp.int32, (32, B), 0)
    pc = lax.broadcasted_iota(jnp.int32, (32, B), 1)
    for jb in range(8):
        between(jb)
        j = 32 * jb
        R = [[T[j + 8 * g:j + 8 * g + 8, 128 * l:128 * l + 128] for l in range(2)] for g in range(4)]
        R = panel(R, j, sub, lane)
        rows = jnp.concatenate([jnp.concatenate(r, axis=1) for r in R], axis=0)
        T[j:j + 32, :] = rows
        if jb < 7:
            left = rows.T[j + 32:, :]
            n = B - j - 32
            ln = lax.broadcasted_iota(jnp.int32, (n, B), 1)
            low = jnp.where((ln >= j) & (ln < j + 32), 0.0, T[j + 32:, :])
            rows = jnp.where((pc < j + 32) & (pc > j + pr), 0.0, rows)
            T[j + 32:, :] = low - dot3(left, rows)


HA = 144
HB = B - HA


def main_kernel(a_ref, bulk, whi_ref, wlo_ref, l_ref,
                at, m_ref, g_ref, S, T, W,
                rg, rm, so, sf, st, rt, ss, ra, rah, rb, rbh, saz, sax, sbx, sbz):
    p = lax.axis_index("prow")
    q = lax.axis_index("pcol")
    x = q // 8
    z = q % 8
    par = p % 2
    sib = p + 1 - 2 * par

    def zat(d):
        return 8 * x + lax.rem(z + d + 16, 8)

    def xat(d):
        return lax.rem(q + 8 * d + 64, 32)

    barrier = pltpu.get_barrier_semaphore()

    def greet(pp, qq):
        pl.semaphore_signal(barrier, inc=1, device_id=(pp, qq), device_id_type=MESH)

    for d in range(1, 8):
        greet(lax.rem(p + d, 8), q)
    for d in (1, 2, 3):
        greet(p, xat(d))
    for d in (1, -1):
        greet(p, zat(d))
    from_p, from_q = z % 4, 8 * x + p
    from_self = (from_p == p) & (from_q == q)

    @pl.when(jnp.logical_not(from_self))
    def _():
        greet(from_p, from_q)

    def scatter_to(c):
        return z, 8 * x + 4 * c + p

    def scatter_self(c):
        return (z == p) & (z == 4 * c + p)

    for c in range(2):
        @pl.when((p < NP) & jnp.logical_not(scatter_self(c)))
        def _():
            greet(*scatter_to(c))
    count = 12 + jnp.where(from_self, 0, 1)
    for c in range(2):
        count = count + jnp.where((p < NP) & jnp.logical_not(scatter_self(c)), 1, 0)
    pl.semaphore_wait(barrier, count)

    def send(src, dst, ssem, rsem, pp, qq):
        return pltpu.make_async_remote_copy(
            src_ref=src, dst_ref=dst, send_sem=ssem, recv_sem=rsem,
            device_id=(pp, qq), device_id_type=MESH,
        )

    def tile(i):
        return pl.ds(pl.multiple_of(i * B, B), B)

    def gslot(k, c):
        return g_ref.at[tile(k), pl.ds(c * B, B)]

    def origin(c):
        for n, d in enumerate((2, 6, 4, None)):
            pp = sib if d is None else lax.rem(p + d, 8)
            yield send(a_ref.at[c], gslot(p, c), so.at[c, n], rg.at[p, c], pp, q)

    def relay(k, c):
        return send(gslot(k, c), gslot(k, c), sf.at[k, c], rg.at[k, c], sib, q)

    def relay_event(i, c):
        k = par + 2 * i

        @pl.when(k != p)
        def _():
            relay(k, c).wait_recv()
            relay(k, c).start()

    def tile_sends(i, kc):
        k = par + 2 * i
        d = lax.rem(z + 8 - kc, 8)
        slot = m_ref.at[tile(k), pl.ds(kc * B, B)]
        rsem = rm.at[k, kc]
        out = []
        for n, dx in enumerate((1, 3, 2)):
            out.append(((d == 0) & (x == 0), send(slot, slot, st.at[i, kc, n], rsem, p, xat(dx))))
        out.append((d < 4, send(slot, slot, st.at[i, kc, 3], rsem, p, zat(1))))
        out.append(((d == 0) | (d > 5), send(slot, slot, st.at[i, kc, 4], rsem, p, zat(-1))))
        out.append((None, send(slot, slot, st.at[i, kc, 5], rsem, sib, q)))
        return d, out

    def tile_event(i, kc):
        k = par + 2 * i

        @pl.when(k <= kc)
        def _():
            d, sends = tile_sends(i, kc)
            here = (d == 0) & (x == 0)

            @pl.when(here)
            def _():
                m_ref[tile(k), kc * B:(kc + 1) * B] = g_ref[tile(k), 0:B]

            @pl.when(jnp.logical_not(here))
            def _():
                sends[5][1].wait_recv()
            for cond, cp in sends:
                if cond is None:
                    cp.start()
                else:
                    pl.when(cond)(cp.start)

    def sibling_tile(k, kc):
        slot = m_ref.at[tile(k), pl.ds(kc * B, B)]
        return send(slot, slot, st.at[0, kc, 5], rm.at[k, kc], sib, q)

    s = 1 - 2 * par

    def scatter(c):
        pp, qq = scatter_to(c)
        return send(at.at[c], bulk.at[qq], ss.at[c], rt.at[0], pp, qq)

    def arrive():
        return send(bulk.at[q], bulk.at[q], ss.at[0], rt.at[0], from_p, from_q)

    def part(t, lo, n):
        return bulk.at[t, pl.ds(lo, n), :]

    def hop(t, lo, n, ssem, rsem, to):
        return send(part(t, lo, n), part(t, lo, n), ssem, rsem, p, to)

    def az(n, way):
        w = s * way
        t = zat(-n * w)
        return hop(t, 0, HA, saz.at[n if way > 0 else 4 + n], ra.at[t], zat(w))

    def bz(dx, n, way):
        w = s * way
        t = 8 * lax.rem(x + dx + 4, 4) + lax.rem(z - n * w + 16, 8)
        return hop(t, HA, HB, sbz.at[dx % 4, n if way > 0 else 4 + n], rb.at[t], zat(w))

    def ax(dz, way):
        t = zat(dz)
        return hop(t, 0, HA, sax.at[dz % 8, 0 if way > 0 else 1], ra.at[t], xat(way))

    def axf(dz, way):
        zz = lax.rem(z + dz + 16, 8)
        t = 8 * lax.rem(x - way + 4, 4) + zz
        h = 0 if way > 0 else 1
        return hop(t, h * (HA // 2), HA // 2, sax.at[dz % 8, 2 + h], rah.at[zz, h], xat(way))

    def bx(way):
        return hop(q, HA, HB, sbx.at[0 if way > 0 else 1], rb.at[q], xat(way))

    def bxf(way):
        h = 0 if way > 0 else 1
        return hop(xat(-way), HA + h * (HB // 2), HB // 2, sbx.at[2 + h], rbh.at[h], xat(way))

    def got(t, lo, n, rsem):
        hop(t, lo, n, saz.at[0], rsem, xat(1)).wait_recv()

    def got_a(t):
        got(t, 0, HA, ra.at[t])

    def got_b(t):
        got(t, HA, HB, rb.at[t])

    def last(way):
        return 4 if way > 0 else 3

    def start_event():
        @pl.when(from_self)
        def _():
            bulk[q] = at[0]

        @pl.when(jnp.logical_not(from_self))
        def _():
            arrive().wait_recv()
        for way in (1, -1):
            az(0, way).start()
            bx(way).start()
            bz(0, 0, way).start()
        for way in (1, -1):
            ax(0, way).start()

    def az_event(n):
        for way in (1, -1):
            if n <= last(way):
                got_a(zat(-n * s * way))
                if n < last(way):
                    az(n, way).start()
        for dz in ((n, -n) if n < 4 else (4,)):
            for way in (1, -1):
                ax(dz, way).start()

    def bx_event():
        for way in (1, -1):
            got_b(xat(-way))
            bxf(way).start()
        for dx in (1, -1):
            for way in (1, -1):
                bz(dx, 0, way).start()

    def bx2_event():
        for h in range(2):
            got(xat(2), HA + h * (HB // 2), HB // 2, rbh.at[h])
        for way in (1, -1):
            bz(2, 0, way).start()

    def bz_event(dx, n):
        for way in (1, -1):
            if n <= last(way):
                got_b(8 * lax.rem(x + dx + 4, 4) + lax.rem(z - n * s * way + 16, 8))
                if n < last(way):
                    bz(dx, n, way).start()

    def ax_event(dz):
        zz = lax.rem(z + dz + 16, 8)
        for way in (1, -1):
            got_a(8 * lax.rem(x - way + 4, 4) + zz)
            axf(dz, way).start()

    def ax2_event(dz):
        zz = lax.rem(z + dz + 16, 8)
        t = 8 * lax.rem(x + 2, 4) + zz
        for h in range(2):
            got(t, h * (HA // 2), HA // 2, rah.at[zz, h])

    E = functools.partial
    xs = (0, 1, -1, 2)
    events = {
        (0, 0): [E(tile_event, 0, 1)],
        (0, 1): [E(tile_event, 0, 2)],
        (0, 2): [E(tile_event, 0, 3)],
        (0, 3): [E(relay_event, 1, 0), bx_event],
        (0, 4): [E(az_event, 1)],
        (0, 5): [E(tile_event, 1, 2)],
        (0, 6): [E(tile_event, 1, 3)],
        (0, 7): [bx2_event],
        (1, 0): [E(az_event, 2)],
        (1, 1): [E(bz_event, 0, 1)],
        (1, 2): [E(bz_event, 1, 1)],
        (1, 3): [E(bz_event, -1, 1)],
        (1, 4): [E(az_event, 3)],
        (1, 5): [E(bz_event, 2, 1)],
        (1, 6): [E(az_event, 4)],
        (1, 7): [E(ax_event, 0)],
        (2, 0): [E(bz_event, 0, 2)],
        (2, 1): [E(bz_event, 1, 2)],
        (2, 2): [E(bz_event, -1, 2)],
        (2, 3): [E(bz_event, 2, 2)],
        (2, 4): [E(ax_event, 1), E(ax_event, -1)],
        (2, 5): [E(ax_event, 2), E(ax_event, -2)],
        (2, 6): [E(bz_event, 0, 3), E(bz_event, 1, 3)],
        (2, 7): [E(bz_event, -1, 3), E(bz_event, 2, 3)],
        (3, 0): [E(ax_event, 3), E(ax_event, -3)],
        (3, 1): [E(ax_event, 4)],
    }

    @pl.when(p < NP)
    def _():
        for cp in origin(0):
            cp.start()
        at[0] = a_ref[0].T
        at[1] = a_ref[1].T
        for c in range(2):
            pl.when(jnp.logical_not(scatter_self(c)))(scatter(c).start)
        for cp in origin(1):
            cp.start()
        for c in range(2):
            g_ref[tile(p), c * B:(c + 1) * B] = a_ref[c]
    relay_event(0, 0)
    tile_event(0, 0)
    start_event()
    S[...] = jnp.zeros_like(S)

    row = lax.broadcasted_iota(jnp.int32, (B, B), 0)
    col = lax.broadcasted_iota(jnp.int32, (B, B), 1)

    def step(k, _):
        other = lax.rem(k, 2) != par

        @pl.when(other)
        def _():
            slot = m_ref.at[tile(k), tile(k)]
            send(slot, slot, st.at[0, 0, 5], rm.at[k, k], sib, q).wait_recv()

        T[...] = S[tile(k), tile(k)] + m_ref[tile(k), tile(k)]

        def between(jb):
            for kk in range(NP):
                for ev in events.get((kk, jb), ()):
                    pl.when(k == kk)(ev)

        factor_tile(T, between)
        S[tile(k), tile(k)] = T[...]
        X = jnp.where(row >= col, T[...], 0.0)
        for kc in range(1, NP):
            pl.when(other & (k < kc))(sibling_tile(k, kc).wait_recv)

        def solve(m, _):
            S[tile(k), tile(m)] = dot3(X, S[tile(k), tile(m)] + m_ref[tile(k), tile(m)])
            return 0

        lax.fori_loop(k + 1, NP, solve, 0)

        @pl.when(k == 0)
        def _():
            relay_event(0, 1)
            relay_event(1, 1)

        for c in range(2):
            @pl.when(other)
            def _():
                relay(k, c).wait_recv()
            S[tile(k), TOP + c * B:TOP + (c + 1) * B] = dot3(
                X, S[tile(k), TOP + c * B:TOP + (c + 1) * B] + g_ref[tile(k), c * B:(c + 1) * B])

        def trail(i, _):
            left = S[tile(k), tile(i)].T

            def inner(m, _):
                S[tile(i), tile(m)] = S[tile(i), tile(m)] - dot3(left, S[tile(k), tile(m)])
                return 0

            lax.fori_loop(i, NP + 2, inner, 0)
            return 0

        lax.fori_loop(k + 1, NP, trail, 0)
        return 0

    lax.fori_loop(0, NP, step, 0)

    kq = jnp.minimum(q, NP - 1)
    kp = jnp.minimum(p, NP - 1)
    u = S[tile(kq), tile(kp)]
    u_diag = jnp.where(col > row, u, jnp.where(col == row, 1.0 / u, 0.0))
    u = jnp.where(kp == kq, u_diag, jnp.where(kq < kp, u, 0.0))
    l_ref[...] = u.T

    col2 = lax.broadcasted_iota(jnp.int32, (B, 2 * B), 1)
    row2 = lax.broadcasted_iota(jnp.int32, (B, 2 * B), 0)
    for k in (3, 2, 1, 0):
        unit = jnp.where((row2 == col2) & (q == k), 1.0, 0.0)
        acc = jnp.where((col2 < B) & (q < NP), unit, S[k * B:(k + 1) * B, TOP:TOP + 2 * B])
        for m in range(k + 1, NP):
            acc = acc - dot3(S[k * B:(k + 1) * B, m * B:(m + 1) * B], W[m * B:(m + 1) * B, :])
        X = jnp.where(row >= col, S[k * B:(k + 1) * B, k * B:(k + 1) * B], 0.0)
        w = dot3(X.T, acc)
        W[k * B:(k + 1) * B, :] = w
        hi, lo = split(w)
        whi_ref[k * B:(k + 1) * B, :] = hi
        wlo_ref[k * B:(k + 1) * B, :] = lo

    for dx in xs:
        bz_event(dx, 4)
    for dz in range(8):
        ax2_event(dz)

    @pl.when(p < NP)
    def _():
        for c in range(2):
            for cp in origin(c):
                cp.wait_send()
            pl.when(jnp.logical_not(scatter_self(c)))(scatter(c).wait_send)
    for c in range(2):
        for i in range(2):
            k = par + 2 * i
            pl.when(k != p)(relay(k, c).wait_send)
    for i in range(2):
        for kc in range(NP):
            @pl.when(par + 2 * i <= kc)
            def _():
                for cond, cp in tile_sends(i, kc)[1]:
                    if cond is None:
                        cp.wait_send()
                    else:
                        pl.when(cond)(cp.wait_send)
    for way in (1, -1):
        bx(way).wait_send()
        bxf(way).wait_send()
        for n in range(last(way)):
            az(n, way).wait_send()
            for dx in xs:
                bz(dx, n, way).wait_send()
        for dz in range(8):
            ax(dz, way).wait_send()
            axf(dz, way).wait_send()


def main(a):
    dma = pltpu.SemaphoreType.DMA
    vmem = pl.BlockSpec(memory_space=pltpu.VMEM)
    return pl.pallas_call(
        main_kernel,
        out_shape=(
            jax.ShapeDtypeStruct((32, B, B), F32),
            jax.ShapeDtypeStruct((TOP, 2 * B), BF16),
            jax.ShapeDtypeStruct((TOP, 2 * B), BF16),
            jax.ShapeDtypeStruct((B, B), F32),
        ),
        in_specs=[vmem],
        out_specs=[vmem] * 4,
        scratch_shapes=[
            pltpu.VMEM((2, B, B), F32),
            pltpu.VMEM((TOP, TOP), F32),
            pltpu.VMEM((TOP, 2 * B), F32),
            pltpu.VMEM((TOP, TOP + 2 * B), F32),
            pltpu.VMEM((B, B), F32),
            pltpu.VMEM((TOP, 2 * B), F32),
            dma((NP, 2)), dma((NP, NP)), dma((2, 4)), dma((NP, 2)), dma((2, NP, 6)),
            dma((1,)), dma((2,)), dma((32,)), dma((8, 2)), dma((32,)), dma((2,)),
            dma((7,)), dma((8, 4)), dma((4,)), dma((4, 7)),
        ],
        compiler_params=pltpu.CompilerParams(
            collective_id=1, has_side_effects=True, vmem_limit_bytes=48 * 1024 * 1024),
        cost_estimate=pl.CostEstimate(
            flops=60_000_000_000, bytes_accessed=8_000_000, transcendentals=0),
        name="main",
    )(a)


def update_kernel(b_ref, m_ref, whi_ref, wlo_ref, l_ref, o_ref):
    r = pl.program_id(0)
    p = lax.axis_index("prow")
    q = lax.axis_index("pcol")
    acc = jnp.zeros((B, 2 * B), F32)
    for k in range(NP):
        left = b_ref[k].astype(BF16)
        acc = acc + dot1(left, whi_ref[k * B:(k + 1) * B, :])
        acc = acc + dot1(left, wlo_ref[k * B:(k + 1) * B, :])
    m = m_ref[0].astype(F32)
    top = (r == 0) & (p < NP)
    factor_col = q < NP
    c0 = jnp.where(factor_col, acc[:, 0:B], m[:, 0:B] - acc[:, 0:B])
    c0 = jnp.where(top, jnp.where(factor_col, l_ref[...], 0.0), c0)
    c1 = jnp.where(top, 0.0, m[:, B:] - acc[:, B:])
    for n, part in enumerate((c0[:, :128], c0[:, 128:], c1[:, :128], c1[:, 128:])):
        o_ref[pl.ds(n, B, stride=4), :] = part


def update(bulk, mine, whi, wlo, ltile):
    return pl.pallas_call(
        update_kernel,
        grid=(8,),
        out_shape=jax.ShapeDtypeStruct((8 * 4 * B, 128), F32),
        in_specs=[
            pl.BlockSpec((4, B, B), lambda r: (2 * (r % 4) + r // 4, 0, 0)),
            pl.BlockSpec((1, B, 2 * B), lambda r: (r, 0, 0)),
            pl.BlockSpec((TOP, 2 * B), lambda r: (0, 0)),
            pl.BlockSpec((TOP, 2 * B), lambda r: (0, 0)),
            pl.BlockSpec((B, B), lambda r: (0, 0)),
        ],
        out_specs=pl.BlockSpec((4 * B, 128), lambda r: (r, 0)),
        compiler_params=pltpu.CompilerParams(vmem_limit_bytes=32 * 1024 * 1024),
        cost_estimate=pl.CostEstimate(
            flops=4_300_000_000, bytes_accessed=16_000_000, transcendentals=0),
        name="update",
    )(bulk, mine, whi, wlo, ltile)


def local(covariance):
    mine = covariance.reshape(8, B, 2, B)
    a = mine[0].astype(F32).transpose(1, 0, 2)
    mine = mine.reshape(8, B, 2 * B)
    bulk, whi, wlo, ltile = main(a)
    out = update(bulk, mine, whi, wlo, ltile)
    return out.reshape(8, 1, B, 2, 1, B)


def solution(mesh):
    in_specs = (P(None, "prow", None, None, "pcol", None),)
    out_specs = P(None, "prow", None, None, "pcol", None)
    return jax.shard_map(local, mesh=mesh, in_specs=in_specs, out_specs=out_specs, check_vma=False)
```

```python
import functools
import jax
import jax.numpy as jnp
from jax import lax
from jax.experimental import pallas as pl
from jax.experimental.pallas import tpu as pltpu
from jax.sharding import PartitionSpec as P

B = 256
NP = 4
TOP = NP * B
F32 = jnp.float32
BF16 = jnp.bfloat16
MESH = pl.DeviceIdType.MESH


def split(a):
    hi = a.astype(BF16)
    return hi, (a - hi.astype(F32)).astype(BF16)


def dot1(a, b):
    return jnp.dot(a, b, preferred_element_type=F32)


def dot3(a, b):
    ah, al = split(a)
    bh, bl = split(b)
    return dot1(ah, bh) + (dot1(ah, bl) + dot1(al, bh))


def panel(R, j, sub, lane):
    for g in range(4):
        c0 = j + 8 * g
        lt = c0 // 128
        o = c0 % 128
        cb = {}
        for h in range(g, 4):
            for t in range(8):
                cb[h, t] = jnp.broadcast_to(R[h][lt][:, o + t:o + t + 1], (8, 128))
        inblk = (lane >= o) & (lane < o + 8)
        R[g][lt] = jnp.where(inblk, jnp.where(lane - o == sub, 1.0, 0.0), R[g][lt])
        for h in range(g + 1, 4):
            R[h][lt] = jnp.where(inblk, 0.0, R[h][lt])
        scale = jnp.zeros((8, 128), F32)
        for t in range(8):
            piv = jnp.broadcast_to(cb[g, t][t:t + 1, :], (8, 128))
            inv = 1.0 / piv
            scale = jnp.where(sub == t, lax.rsqrt(piv), scale)
            rows = [jnp.broadcast_to(R[g][l][t:t + 1, :], (8, 128)) for l in range(2)]
            crow = {u: jnp.broadcast_to(cb[g, u][t:t + 1, :], (8, 128)) for u in range(t + 1, 8)}
            for h in range(g, 4):
                f = cb[h, t] * inv
                if h == g:
                    f = jnp.where(sub > t, f, 0.0)
                for l in range(2):
                    R[h][l] = R[h][l] - f * rows[l]
                for u in range(t + 1, 8):
                    cb[h, u] = cb[h, u] - f * crow[u]
        for u in range(1, 8):
            R[g][lt] = jnp.where((lane == o + u) & (sub < u), cb[g, u], R[g][lt])
        for l in range(2):
            R[g][l] = R[g][l] * scale
    return R


def factor_tile(T, between):
    sub = lax.broadcasted_iota(jnp.int32, (8, 128), 0)
    lane = lax.broadcasted_iota(jnp.int32, (8, 128), 1)
    pr = lax.broadcasted_iota(jnp.int32, (32, B), 0)
    pc = lax.broadcasted_iota(jnp.int32, (32, B), 1)
    for jb in range(8):
        between(jb)
        j = 32 * jb
        R = [[T[j + 8 * g:j + 8 * g + 8, 128 * l:128 * l + 128] for l in range(2)] for g in range(4)]
        R = panel(R, j, sub, lane)
        rows = jnp.concatenate([jnp.concatenate(r, axis=1) for r in R], axis=0)
        T[j:j + 32, :] = rows
        if jb < 7:
            left = rows.T[j + 32:, :]
            n = B - j - 32
            ln = lax.broadcasted_iota(jnp.int32, (n, B), 1)
            low = jnp.where((ln >= j) & (ln < j + 32), 0.0, T[j + 32:, :])
            rows = jnp.where((pc < j + 32) & (pc > j + pr), 0.0, rows)
            T[j + 32:, :] = low - dot3(left, rows)


HA = 176
HB = B - HA


def main_kernel(a_ref, bulk, whi_ref, wlo_ref, l_ref,
                at, m_ref, g_ref, S, T, W,
                rg, so, sf, r1, r2, r3, r4, r5, s1, s2, s2b, s3, s4, s5,
                rt, ss, ra, rah, rb, saz, sax, sbx, sbz):
    p = lax.axis_index("prow")
    q = lax.axis_index("pcol")
    x = q // 8
    z = q % 8
    par = p % 2
    sib = p + 1 - 2 * par

    def zat(d):
        return 8 * x + lax.rem(z + d + 16, 8)

    def xat(d):
        return lax.rem(q + 8 * d + 64, 32)

    barrier = pltpu.get_barrier_semaphore()

    def greet(pp, qq):
        pl.semaphore_signal(barrier, inc=1, device_id=(pp, qq), device_id_type=MESH)

    y = p // 2
    for d in range(1, 8):
        greet(lax.rem(p + d, 8), q)
        greet(p, zat(d))
    for d in (1, 2, 3):
        greet(p, xat(d))
    count = jnp.int32(17)

    from_p, from_q = lax.rem(z - p + 8, 4), 8 * x + p
    from_self = (p == 0) & (z == 0)

    def scatter_to(c):
        return z, 8 * x + lax.rem(z + 4 * c + p, 8)

    def scatter_self(c):
        return (p == 0) & (z == 0) & (c == 0)

    def greet_if(cond, pp, qq):
        pl.when(cond)(functools.partial(greet, pp, qq))
        return jnp.where(cond, 1, 0)

    count = count + greet_if(jnp.logical_not(from_self), from_p, from_q)
    for c in range(2):
        count = count + greet_if((p < NP) & jnp.logical_not(scatter_self(c)), *scatter_to(c))

    tiles = ((0, 0, 0), (0, 1, 0), (0, 2, 1), (0, 3, 2), (1, 1, 3),
             (1, 2, 0), (1, 3, 1), (2, 2, 2), (2, 3, 3), (3, 3, 0))
    origin_dev = (p < NP) & (p <= q) & (q < NP)
    plane = jnp.int32(0)
    my_tile = jnp.int32(0)
    for t, (k, kc, yt) in enumerate(tiles):
        me = (p == k) & (q == kc)
        plane = jnp.where(me, yt, plane)
        my_tile = jnp.where(me, t, my_tile)
        count = count + greet_if((x == 0) & (y == yt) & jnp.logical_not(me), k, kc)

    def piece_targets():
        for c in range(2):
            for d in range(8):
                yield c, d, (2 * plane + c), lax.rem(z + d, 8)

    for c, d, pp, qq in piece_targets():
        cond = origin_dev & jnp.logical_not((p == pp) & (q == qq))
        count = count + greet_if(cond, pp, qq)
    relay0 = (x == 0) & (y == 0)
    count = count + greet_if(jnp.logical_not(relay0), par, z)

    def relay_targets():
        for dy in range(4):
            for dx in range(4):
                if dx or dy:
                    yield 4 * dy + dx, 2 * lax.rem(y + dy, 4) + par, xat(dx)

    for _, pp, qq in relay_targets():
        count = count + greet_if(relay0, pp, qq)
    pl.semaphore_wait(barrier, count)

    def send(src, dst, ssem, rsem, pp, qq):
        return pltpu.make_async_remote_copy(
            src_ref=src, dst_ref=dst, send_sem=ssem, recv_sem=rsem,
            device_id=(pp, qq), device_id_type=MESH,
        )

    def tile(i):
        return pl.ds(pl.multiple_of(i * B, B), B)

    def gslot(k, c):
        return g_ref.at[tile(k), pl.ds(c * B, B)]

    def origin(c):
        for n, d in enumerate((2, 6, 4, None)):
            pp = sib if d is None else lax.rem(p + d, 8)
            yield send(a_ref.at[c], gslot(p, c), so.at[c, n], rg.at[p, c], pp, q)

    def relay(k, c):
        return send(gslot(k, c), gslot(k, c), sf.at[k, c], rg.at[k, c], sib, q)

    def relay_event(i, c):
        k = par + 2 * i

        @pl.when(k != p)
        def _():
            relay(k, c).wait_recv()
            relay(k, c).start()

    def mpart(t, lo, n):
        k, kc, _ = tiles[t]
        return m_ref.at[pl.ds(pl.multiple_of(k * B + lo, 16), n), pl.ds(kc * B, B)]

    def one_piece(c, d, pp, qq):
        lo = pl.multiple_of(c * 128 + 16 * qq, 16)
        dst = m_ref.at[pl.ds(pl.multiple_of(p * B + c * 128 + 16 * qq, 16), 16), tile(q)]
        return send(a_ref.at[0, pl.ds(lo, 16), :], dst, s1.at[c, d], r1.at[my_tile], pp, qq)

    def each_piece(act):
        for c, d, pp, qq in piece_targets():
            cp = one_piece(c, d, pp, qq)
            if d == 0:
                pl.when((p != pp))(functools.partial(act, cp))
            else:
                act(cp)

    my_lo = par * 128 + 16 * z

    def my_piece(t):
        return mpart(t, my_lo, 16)

    def got_piece(t, ref, rsem):
        send(ref, ref, s1.at[0, 0], rsem, sib, q).wait_recv()

    def relay_sends(t):
        if t == 0:
            for n, pp, qq in relay_targets():
                yield send(my_piece(t), my_piece(t), s2.at[n], r2.at[t], pp, qq)
        else:
            for n in range(3):
                yield send(my_piece(t), my_piece(t), s2b.at[t, n], r2.at[t], p, xat(n + 1))

    def relay_tile(t):
        k, kc, yt = tiles[t]

        @pl.when((x == 0) & (y == yt))
        def _():
            @pl.when(jnp.logical_not((p == k) & (q == kc)))
            def _():
                got_piece(t, my_piece(t), r1.at[t])
            for cp in relay_sends(t):
                cp.start()

    def in_plane(t):
        return None if t == 0 else y == tiles[t][2]

    def when(cond, f):
        if cond is None:
            f()
        else:
            pl.when(cond)(f)

    def ring_send(t, d):
        return send(my_piece(t), my_piece(t), s3.at[t, d], r3.at[t, z], p, zat(d))

    def ring_tile(t):
        def go():
            @pl.when(jnp.logical_not((x == 0) & (y == tiles[t][2])))
            def _():
                got_piece(t, my_piece(t), r2.at[t])
            for d in (4, 3, 5, 2, 6, 1, 7):
                ring_send(t, d).start()
        when(in_plane(t), go)

    def half_send(t, c):
        part = mpart(t, c * 128, 128)
        return send(part, part, s4.at[t], r4.at[t], sib, q)

    def plane_sends(t):
        part = mpart(t, par * 128, 128)
        for n in range(3):
            yield send(part, part, s5.at[t, n], r5.at[t], lax.rem(p + 2 * n + 2, 8), q)

    def half_tile(t):
        def go():
            for d in range(1, 8):
                w = lax.rem(z + d, 8)
                got_piece(t, mpart(t, par * 128 + 16 * w, 16), r3.at[t, w])
            if t:
                for cp in plane_sends(t):
                    cp.start()
            half_send(t, par).start()
        when(in_plane(t), go)

    def pass_tile(t):
        @pl.when(y != tiles[t][2])
        def _():
            got_piece(t, mpart(t, par * 128, 128), r5.at[t])
            half_send(t, par).start()

    def half_got(t):
        half_send(t, 1 - par).wait_recv()

    s = 1 - 2 * par

    def scatter(c):
        pp, qq = scatter_to(c)
        return send(at.at[c], bulk.at[qq], ss.at[c], rt.at[0], pp, qq)

    def arrive():
        return send(bulk.at[q], bulk.at[q], ss.at[0], rt.at[0], from_p, from_q)

    def part(t, lo, n):
        return bulk.at[t, pl.ds(lo, n), :]

    def hop(t, lo, n, ssem, rsem, to):
        return send(part(t, lo, n), part(t, lo, n), ssem, rsem, p, to)

    def az(n, way):
        w = s * way
        t = zat(-n * w)
        return hop(t, 0, HA, saz.at[n if way > 0 else 4 + n], ra.at[t], zat(w))

    def bz(dx, n, way):
        w = s * way
        t = 8 * lax.rem(x + dx + 4, 4) + lax.rem(z - n * w + 16, 8)
        return hop(t, HA, HB, sbz.at[dx % 4, n if way > 0 else 4 + n], rb.at[t], zat(w))

    def ax(dz, way):
        t = zat(dz)
        return hop(t, 0, HA, sax.at[dz % 8, 0 if way > 0 else 1], ra.at[t], xat(way))

    def axf(dz, way):
        zz = lax.rem(z + dz + 16, 8)
        t = 8 * lax.rem(x - way + 4, 4) + zz
        h = 0 if way > 0 else 1
        return hop(t, h * (HA // 2), HA // 2, sax.at[dz % 8, 2 + h], rah.at[zz, h], xat(way))

    def bx(n):
        return hop(q, HA, HB, sbx.at[n], rb.at[q], xat(n + 1))

    def got(t, lo, n, rsem):
        hop(t, lo, n, saz.at[0], rsem, xat(1)).wait_recv()

    def got_a(t):
        got(t, 0, HA, ra.at[t])

    def got_b(t):
        got(t, HA, HB, rb.at[t])

    def last(way):
        return 4 if way > 0 else 3

    def start_event():
        @pl.when(from_self)
        def _():
            cp = pltpu.make_async_copy(at.at[0], bulk.at[q], rt.at[0])
            cp.start()
            cp.wait()

        @pl.when(jnp.logical_not(from_self))
        def _():
            arrive().wait_recv()
        for n in (0, 2, 1):
            bx(n).start()
        for way in (1, -1):
            az(0, way).start()
            bz(0, 0, way).start()
        for way in (1, -1):
            ax(0, way).start()

    def az_event(n):
        for way in (1, -1):
            if n <= last(way):
                got_a(zat(-n * s * way))
                if n < last(way):
                    az(n, way).start()
        for dz in ((n, -n) if n < 4 else (4,)):
            for way in (1, -1):
                ax(dz, way).start()

    def bx_event():
        for dx in (1, -1, 2):
            got_b(xat(dx))
            for way in (1, -1):
                bz(dx, 0, way).start()

    def bz_event(dx, n):
        for way in (1, -1):
            if n <= last(way):
                got_b(8 * lax.rem(x + dx + 4, 4) + lax.rem(z - n * s * way + 16, 8))
                if n < last(way):
                    bz(dx, n, way).start()

    def ax_event(dz):
        zz = lax.rem(z + dz + 16, 8)
        for way in (1, -1):
            got_a(8 * lax.rem(x - way + 4, 4) + zz)
            axf(dz, way).start()

    def ax2_event(dz):
        zz = lax.rem(z + dz + 16, 8)
        t = 8 * lax.rem(x + 2, 4) + zz
        for h in range(2):
            got(t, h * (HA // 2), HA // 2, rah.at[zz, h])

    E = functools.partial
    xs = (0, 1, -1, 2)
    def strips_event():
        @pl.when(p < NP)
        def _():
            for c in range(2):
                for cp in origin(c):
                    cp.start()
                g_ref[tile(p), c * B:(c + 1) * B] = a_ref[c]

    events = {
        (0, 0): [E(half_tile, t) for t in (1, 2, 3, 4)] + [E(ring_tile, t) for t in (5, 6, 7, 8)],
        (0, 2): [start_event],
        (0, 3): [E(half_tile, t) for t in (5, 6, 7, 8)],
        (0, 4): [E(pass_tile, t) for t in (1, 2, 3, 4)] + [E(ring_tile, 9)],
        (0, 5): [bx_event],
        (0, 6): [E(az_event, 1)],
        (0, 7): [E(pass_tile, t) for t in (5, 6, 7, 8)] + [E(half_tile, 9)],
        (1, 0): [E(bz_event, 0, 1), strips_event],
        (1, 1): [E(az_event, 2), E(pass_tile, 9)],
        (1, 2): [E(bz_event, 1, 1), E(bz_event, -1, 1)],
        (1, 3): [E(bz_event, 2, 1)],
        (1, 4): [E(az_event, 3)],
        (1, 5): [E(bz_event, 0, 2)],
        (1, 6): [E(ax_event, 0), E(ax_event, 1), E(ax_event, -1)],
        (1, 7): [E(az_event, 4), E(bz_event, 1, 2), E(bz_event, -1, 2)],
        (2, 0): [E(bz_event, 2, 2)],
        (2, 2): [E(bz_event, 0, 3), E(ax_event, 2), E(ax_event, -2)],
        (2, 4): [E(bz_event, 1, 3), E(bz_event, -1, 3)],
        (2, 6): [E(bz_event, 2, 3), E(ax_event, 3), E(ax_event, -3)],
        (3, 0): [E(ax_event, 4)],
        (3, 2): [E(relay_event, 0, 0), E(relay_event, 1, 0)],
        (3, 4): [E(relay_event, 0, 1), E(relay_event, 1, 1)],
    }

    def scatter_start():
        at[0] = a_ref[0].T
        at[1] = a_ref[1].T
        for c in range(2):
            pl.when(jnp.logical_not(scatter_self(c)))(scatter(c).start)

    @pl.when(origin_dev)
    def _():
        each_piece(lambda cp: cp.start())

        @pl.when(plane == y)
        def _():
            lo = pl.multiple_of(my_lo, 16)
            m_ref[pl.ds(pl.multiple_of(p * B + my_lo, 16), 16), tile(q)] = a_ref[0, pl.ds(lo, 16), :]
    pl.when((p < NP) & (x != 0))(scatter_start)
    for t in range(10):
        relay_tile(t)
    pl.when((p < NP) & (x == 0))(scatter_start)
    ring_tile(0)
    for t in (1, 2, 3, 4):
        ring_tile(t)
    S[...] = jnp.zeros_like(S)
    half_tile(0)

    row = lax.broadcasted_iota(jnp.int32, (B, B), 0)
    col = lax.broadcasted_iota(jnp.int32, (B, B), 1)

    def step(k, _):
        for t, (kk, kc, _) in enumerate(tiles):
            if kk == kc:
                pl.when(k == kk)(functools.partial(half_got, t))

        T[...] = S[tile(k), tile(k)] + m_ref[tile(k), tile(k)]

        def between(jb):
            for kk in range(NP):
                for ev in events.get((kk, jb), ()):
                    pl.when(k == kk)(ev)

        factor_tile(T, between)
        S[tile(k), tile(k)] = T[...]
        X = jnp.where(row >= col, T[...], 0.0)
        for t, (kk, kc, _) in enumerate(tiles):
            if kk != kc:
                pl.when(k == kk)(functools.partial(half_got, t))

        def solve(m, _):
            S[tile(k), tile(m)] = dot3(X, S[tile(k), tile(m)] + m_ref[tile(k), tile(m)])
            return 0

        lax.fori_loop(k + 1, NP, solve, 0)

        def trail(i, _):
            left = S[tile(k), tile(i)].T

            def inner(m, _):
                S[tile(i), tile(m)] = S[tile(i), tile(m)] - dot3(left, S[tile(k), tile(m)])
                return 0

            lax.fori_loop(i, NP, inner, 0)
            return 0

        lax.fori_loop(k + 1, NP, trail, 0)
        return 0

    lax.fori_loop(0, NP, step, 0)

    for i in range(2):
        for c in range(2):
            relay(1 - par + 2 * i, c).wait_recv()

    def block(i, j):
        return S[i * B:(i + 1) * B, j * B:(j + 1) * B]

    for k in range(NP):
        acc = g_ref[k * B:(k + 1) * B, :]
        for i in range(k):
            acc = acc - dot3(block(i, k).T, W[i * B:(i + 1) * B, :])
        W[k * B:(k + 1) * B, :] = dot3(jnp.where(row >= col, block(k, k), 0.0), acc)

    kq = jnp.minimum(q, NP - 1)
    kp = jnp.minimum(p, NP - 1)
    u = S[tile(kq), tile(kp)]
    u_diag = jnp.where(col > row, u, jnp.where(col == row, 1.0 / u, 0.0))
    u = jnp.where(kp == kq, u_diag, jnp.where(kq < kp, u, 0.0))
    l_ref[...] = u.T

    col2 = lax.broadcasted_iota(jnp.int32, (B, 2 * B), 1)
    row2 = lax.broadcasted_iota(jnp.int32, (B, 2 * B), 0)
    for k in (3, 2, 1, 0):
        unit = jnp.where((row2 == col2) & (q == k), 1.0, 0.0)
        acc = jnp.where((col2 < B) & (q < NP), unit, W[k * B:(k + 1) * B, :])
        for m in range(k + 1, NP):
            acc = acc - dot3(S[k * B:(k + 1) * B, m * B:(m + 1) * B], W[m * B:(m + 1) * B, :])
        X = jnp.where(row >= col, S[k * B:(k + 1) * B, k * B:(k + 1) * B], 0.0)
        w = dot3(X.T, acc)
        W[k * B:(k + 1) * B, :] = w
        hi, lo = split(w)
        whi_ref[k * B:(k + 1) * B, :] = hi
        wlo_ref[k * B:(k + 1) * B, :] = lo

    for dx in xs:
        bz_event(dx, 4)
    for dz in range(8):
        ax2_event(dz)

    @pl.when(p < NP)
    def _():
        for c in range(2):
            for cp in origin(c):
                cp.wait_send()
            pl.when(jnp.logical_not(scatter_self(c)))(scatter(c).wait_send)
    for c in range(2):
        for i in range(2):
            k = par + 2 * i
            pl.when(k != p)(relay(k, c).wait_send)
    pl.when(origin_dev)(lambda: each_piece(lambda cp: cp.wait_send()))
    for t in range(10):
        @pl.when((x == 0) & (y == tiles[t][2]))
        def _():
            for cp in relay_sends(t):
                cp.wait_send()

        def drain():
            for d in range(1, 8):
                ring_send(t, d).wait_send()
            if t:
                for cp in plane_sends(t):
                    cp.wait_send()
        when(in_plane(t), drain)
        half_send(t, par).wait_send()
    for n in range(3):
        bx(n).wait_send()
    for way in (1, -1):
        for n in range(last(way)):
            az(n, way).wait_send()
            for dx in xs:
                bz(dx, n, way).wait_send()
        for dz in range(8):
            ax(dz, way).wait_send()
            axf(dz, way).wait_send()


def main(a):
    dma = pltpu.SemaphoreType.DMA
    vmem = pl.BlockSpec(memory_space=pltpu.VMEM)
    return pl.pallas_call(
        main_kernel,
        out_shape=(
            jax.ShapeDtypeStruct((32, B, B), F32),
            jax.ShapeDtypeStruct((TOP, 2 * B), BF16),
            jax.ShapeDtypeStruct((TOP, 2 * B), BF16),
            jax.ShapeDtypeStruct((B, B), F32),
        ),
        in_specs=[vmem],
        out_specs=[vmem] * 4,
        scratch_shapes=[
            pltpu.VMEM((2, B, B), F32),
            pltpu.VMEM((TOP, TOP), F32),
            pltpu.VMEM((TOP, 2 * B), F32),
            pltpu.VMEM((TOP, TOP), F32),
            pltpu.VMEM((B, B), F32),
            pltpu.VMEM((TOP, 2 * B), F32),
            dma((NP, 2)), dma((2, 4)), dma((NP, 2)),
            dma((10,)), dma((10,)), dma((10, 8)), dma((10,)), dma((10,)),
            dma((2, 8)), dma((16,)), dma((10, 3)), dma((10, 8)), dma((10,)), dma((10, 3)),
            dma((1,)), dma((2,)), dma((32,)), dma((8, 2)), dma((32,)),
            dma((7,)), dma((8, 4)), dma((3,)), dma((4, 7)),
        ],
        compiler_params=pltpu.CompilerParams(
            collective_id=1, has_side_effects=True, vmem_limit_bytes=30 * 1024 * 1024),
        cost_estimate=pl.CostEstimate(
            flops=60_000_000_000, bytes_accessed=8_000_000, transcendentals=0),
        name="main",
    )(a)


def update_kernel(p_ref, b0, b1, b2, b3, m_ref, whi_ref, wlo_ref, l_ref, o_ref):
    r = pl.program_id(0)
    p = p_ref[0]
    q = p_ref[1]
    acc = jnp.zeros((B, 2 * B), F32)
    for k, b_ref in enumerate((b0, b1, b2, b3)):
        left = b_ref[0].astype(BF16)
        acc = acc + dot1(left, whi_ref[k * B:(k + 1) * B, :])
        acc = acc + dot1(left, wlo_ref[k * B:(k + 1) * B, :])
    m = m_ref[0].astype(F32)
    top = (r == 0) & (p < NP)
    factor_col = q < NP
    c0 = jnp.where(factor_col, acc[:, 0:B], m[:, 0:B] - acc[:, 0:B])
    c0 = jnp.where(top, jnp.where(factor_col, l_ref[...], 0.0), c0)
    c1 = jnp.where(top, 0.0, m[:, B:] - acc[:, B:])
    for n, part in enumerate((c0[:, :128], c0[:, 128:], c1[:, :128], c1[:, 128:])):
        o_ref[pl.ds(n, B, stride=4), :] = part


def update(place, bulk, mine, whi, wlo, ltile):
    def stream(k):
        def index(r, place):
            return 8 * (r % 4) + (place[0] + 4 * (r // 4) + k) % 8, 0, 0
        return pl.BlockSpec((1, B, B), index)

    return pl.pallas_call(
        update_kernel,
        out_shape=jax.ShapeDtypeStruct((8 * 4 * B, 128), F32),
        grid_spec=pltpu.PrefetchScalarGridSpec(
            num_scalar_prefetch=1,
            grid=(8,),
            in_specs=[stream(k) for k in range(NP)] + [
                pl.BlockSpec((1, B, 2 * B), lambda r, place: (r, 0, 0)),
                pl.BlockSpec((TOP, 2 * B), lambda r, place: (0, 0)),
                pl.BlockSpec((TOP, 2 * B), lambda r, place: (0, 0)),
                pl.BlockSpec((B, B), lambda r, place: (0, 0)),
            ],
            out_specs=pl.BlockSpec((4 * B, 128), lambda r, place: (r, 0)),
        ),
        compiler_params=pltpu.CompilerParams(vmem_limit_bytes=20 * 1024 * 1024),
        cost_estimate=pl.CostEstimate(
            flops=4_300_000_000, bytes_accessed=16_000_000, transcendentals=0),
        name="update",
    )(place, bulk, bulk, bulk, bulk, mine, whi, wlo, ltile)


def local(covariance):
    mine = covariance.reshape(8, B, 2, B)
    a = mine[0].astype(F32).transpose(1, 0, 2)
    mine = mine.reshape(8, B, 2 * B)
    bulk, whi, wlo, ltile = main(a)
    place = jnp.stack([lax.axis_index("prow"), lax.axis_index("pcol")]).astype(jnp.int32)
    out = update(place, bulk, mine, whi, wlo, ltile)
    return out.reshape(8, 1, B, 2, 1, B)


def solution(mesh):
    in_specs = (P(None, "prow", None, None, "pcol", None),)
    out_specs = P(None, "prow", None, None, "pcol", None)
    return jax.shard_map(local, mesh=mesh, in_specs=in_specs, out_specs=out_specs, check_vma=False)
```

```python
import functools
import jax
import jax.numpy as jnp
from jax import lax
from jax.experimental import pallas as pl
from jax.experimental.pallas import tpu as pltpu
from jax.sharding import PartitionSpec as P

B = 256
NP = 4
TOP = NP * B
F32 = jnp.float32
BF16 = jnp.bfloat16
MESH = pl.DeviceIdType.MESH


def split(a):
    hi = a.astype(BF16)
    return hi, (a - hi.astype(F32)).astype(BF16)


def dot1(a, b):
    return jnp.dot(a, b, preferred_element_type=F32)


def dot3(a, b):
    ah, al = split(a)
    bh, bl = split(b)
    return dot1(ah, bh) + (dot1(ah, bl) + dot1(al, bh))


def panel(R, j, sub, lane):
    for g in range(4):
        c0 = j + 8 * g
        lt = c0 // 128
        o = c0 % 128
        cb = {}
        for h in range(g, 4):
            for t in range(8):
                cb[h, t] = jnp.broadcast_to(R[h][lt][:, o + t:o + t + 1], (8, 128))
        inblk = (lane >= o) & (lane < o + 8)
        R[g][lt] = jnp.where(inblk, jnp.where(lane - o == sub, 1.0, 0.0), R[g][lt])
        for h in range(g + 1, 4):
            R[h][lt] = jnp.where(inblk, 0.0, R[h][lt])
        scale = jnp.zeros((8, 128), F32)
        for t in range(8):
            piv = jnp.broadcast_to(cb[g, t][t:t + 1, :], (8, 128))
            inv = 1.0 / piv
            scale = jnp.where(sub == t, lax.rsqrt(piv), scale)
            rows = [jnp.broadcast_to(R[g][l][t:t + 1, :], (8, 128)) for l in range(2)]
            crow = {u: jnp.broadcast_to(cb[g, u][t:t + 1, :], (8, 128)) for u in range(t + 1, 8)}
            for h in range(g, 4):
                f = cb[h, t] * inv
                if h == g:
                    f = jnp.where(sub > t, f, 0.0)
                for l in range(2):
                    R[h][l] = R[h][l] - f * rows[l]
                for u in range(t + 1, 8):
                    cb[h, u] = cb[h, u] - f * crow[u]
        for u in range(1, 8):
            R[g][lt] = jnp.where((lane == o + u) & (sub < u), cb[g, u], R[g][lt])
        for l in range(2):
            R[g][l] = R[g][l] * scale
    return R


def factor_tile(T, between):
    sub = lax.broadcasted_iota(jnp.int32, (8, 128), 0)
    lane = lax.broadcasted_iota(jnp.int32, (8, 128), 1)
    pr = lax.broadcasted_iota(jnp.int32, (32, B), 0)
    pc = lax.broadcasted_iota(jnp.int32, (32, B), 1)
    for jb in range(8):
        between(jb)
        j = 32 * jb
        R = [[T[j + 8 * g:j + 8 * g + 8, 128 * l:128 * l + 128] for l in range(2)] for g in range(4)]
        R = panel(R, j, sub, lane)
        rows = jnp.concatenate([jnp.concatenate(r, axis=1) for r in R], axis=0)
        T[j:j + 32, :] = rows
        if jb < 7:
            left = rows.T[j + 32:, :]
            n = B - j - 32
            ln = lax.broadcasted_iota(jnp.int32, (n, B), 1)
            low = jnp.where((ln >= j) & (ln < j + 32), 0.0, T[j + 32:, :])
            rows = jnp.where((pc < j + 32) & (pc > j + pr), 0.0, rows)
            T[j + 32:, :] = low - dot3(left, rows)


HA = 160
HB = B - HA


def main_kernel(a_ref, bulk, whi_ref, wlo_ref, l_ref,
                at, m_ref, g_ref, S, T, W,
                rg, so, sf, sg, r1, r2, r3, r4, r5, s1, s2, s2b, s3, s4, s5,
                rt, ss, ra, rah, rb, saz, sax, sbx, sbz):
    p = lax.axis_index("prow")
    q = lax.axis_index("pcol")
    x = q // 8
    z = q % 8
    par = p % 2
    sib = p + 1 - 2 * par

    def zat(d):
        return 8 * x + lax.rem(z + d + 16, 8)

    def xat(d):
        return lax.rem(q + 8 * d + 64, 32)

    barrier = pltpu.get_barrier_semaphore()

    def greet(pp, qq):
        pl.semaphore_signal(barrier, inc=1, device_id=(pp, qq), device_id_type=MESH)

    y = p // 2
    for d in range(1, 8):
        greet(lax.rem(p + d, 8), q)
        greet(p, zat(d))
    for d in (1, 2, 3):
        greet(p, xat(d))
    count = jnp.int32(17)

    from_p, from_q = lax.rem(z - p + 8, 4), 8 * x + p
    from_self = (p == 0) & (z == 0)

    def scatter_to(c):
        return z, 8 * x + lax.rem(z + 4 * c + p, 8)

    def scatter_self(c):
        return (p == 0) & (z == 0) & (c == 0)

    def greet_if(cond, pp, qq):
        pl.when(cond)(functools.partial(greet, pp, qq))
        return jnp.where(cond, 1, 0)

    count = count + greet_if(jnp.logical_not(from_self), from_p, from_q)
    for c in range(2):
        count = count + greet_if((p < NP) & jnp.logical_not(scatter_self(c)), *scatter_to(c))

    tiles = ((0, 0, 0), (0, 1, 0), (0, 2, 1), (0, 3, 2), (1, 1, 3),
             (1, 2, 0), (1, 3, 1), (2, 2, 2), (2, 3, 3), (3, 3, 0))
    origin_dev = (p < NP) & (p <= q) & (q < NP)
    plane = jnp.int32(0)
    my_tile = jnp.int32(0)
    for t, (k, kc, yt) in enumerate(tiles):
        me = (p == k) & (q == kc)
        plane = jnp.where(me, yt, plane)
        my_tile = jnp.where(me, t, my_tile)
        count = count + greet_if((x == 0) & (y == yt) & jnp.logical_not(me), k, kc)

    def piece_targets():
        for c in range(2):
            for d in range(8):
                yield c, d, (2 * plane + c), lax.rem(z + d, 8)

    for c, d, pp, qq in piece_targets():
        cond = origin_dev & jnp.logical_not((p == pp) & (q == qq))
        count = count + greet_if(cond, pp, qq)
    relay0 = (x == 0) & (y == 0)
    count = count + greet_if(jnp.logical_not(relay0), par, z)

    def relay_targets():
        for dy in range(4):
            for dx in range(4):
                if dx or dy:
                    yield 4 * dy + dx, 2 * lax.rem(y + dy, 4) + par, xat(dx)

    for _, pp, qq in relay_targets():
        count = count + greet_if(relay0, pp, qq)
    pl.semaphore_wait(barrier, count)

    def send(src, dst, ssem, rsem, pp, qq):
        return pltpu.make_async_remote_copy(
            src_ref=src, dst_ref=dst, send_sem=ssem, recv_sem=rsem,
            device_id=(pp, qq), device_id_type=MESH,
        )

    def tile(i):
        return pl.ds(pl.multiple_of(i * B, B), B)

    def gslot(k, c):
        return g_ref.at[tile(k), pl.ds(c * B, B)]

    def origin(c):
        for n, d in enumerate((2, 6, None)):
            pp = sib if d is None else lax.rem(p + d, 8)
            yield send(a_ref.at[c], gslot(p, c), so.at[c, n], rg.at[p, c], pp, q)

    def relay(k, c):
        return send(gslot(k, c), gslot(k, c), sf.at[k, c], rg.at[k, c], sib, q)

    def onward(i, c):
        k = par + 2 * i
        pp = lax.rem(p + (2 if c == 0 else 6), 8)
        return y == (i + (1 if c == 0 else 3)) % 4, send(
            gslot(k, c), gslot(k, c), sg.at[i, c], rg.at[k, c], pp, q)

    def relay_event(i, c, far):
        k = par + 2 * i
        opposite = y == (i + 2) % 4

        @pl.when(opposite if far else (k != p) & jnp.logical_not(opposite))
        def _():
            relay(k, c).wait_recv()
            relay(k, c).start()
            if not far:
                cond, cp = onward(i, c)
                pl.when(cond)(cp.start)

    def mpart(t, lo, n):
        k, kc, _ = tiles[t]
        return m_ref.at[pl.ds(pl.multiple_of(k * B + lo, 16), n), pl.ds(kc * B, B)]

    def one_piece(c, d, pp, qq):
        lo = pl.multiple_of(c * 128 + 16 * qq, 16)
        dst = m_ref.at[pl.ds(pl.multiple_of(p * B + c * 128 + 16 * qq, 16), 16), tile(q)]
        return send(a_ref.at[0, pl.ds(lo, 16), :], dst, s1.at[c, d], r1.at[my_tile], pp, qq)

    def each_piece(act):
        for c, d, pp, qq in piece_targets():
            cp = one_piece(c, d, pp, qq)
            if d == 0:
                pl.when((p != pp))(functools.partial(act, cp))
            else:
                act(cp)

    my_lo = par * 128 + 16 * z

    def my_piece(t):
        return mpart(t, my_lo, 16)

    def got_piece(t, ref, rsem):
        send(ref, ref, s1.at[0, 0], rsem, sib, q).wait_recv()

    def relay_sends(t):
        if t == 0:
            for n, pp, qq in relay_targets():
                yield send(my_piece(t), my_piece(t), s2.at[n], r2.at[t], pp, qq)
        else:
            for n in range(3):
                yield send(my_piece(t), my_piece(t), s2b.at[t, n], r2.at[t], p, xat(n + 1))

    def relay_tile(t):
        k, kc, yt = tiles[t]

        @pl.when((x == 0) & (y == yt))
        def _():
            @pl.when(jnp.logical_not((p == k) & (q == kc)))
            def _():
                got_piece(t, my_piece(t), r1.at[t])
            for cp in relay_sends(t):
                cp.start()

    def in_plane(t):
        return None if t == 0 else y == tiles[t][2]

    def when(cond, f):
        if cond is None:
            f()
        else:
            pl.when(cond)(f)

    def ring_send(t, d):
        return send(my_piece(t), my_piece(t), s3.at[t, d], r3.at[t, z], p, zat(d))

    def ring_tile(t):
        def go():
            @pl.when(jnp.logical_not((x == 0) & (y == tiles[t][2])))
            def _():
                got_piece(t, my_piece(t), r2.at[t])
            for d in (4, 3, 5, 2, 6, 1, 7):
                ring_send(t, d).start()
        when(in_plane(t), go)

    def half_send(t, c):
        part = mpart(t, c * 128, 128)
        return send(part, part, s4.at[t], r4.at[t], sib, q)

    def plane_sends(t):
        part = mpart(t, par * 128, 128)
        for n in range(3):
            yield send(part, part, s5.at[t, n], r5.at[t], lax.rem(p + 2 * n + 2, 8), q)

    def half_tile(t):
        def go():
            for d in range(1, 8):
                w = lax.rem(z + d, 8)
                got_piece(t, mpart(t, par * 128 + 16 * w, 16), r3.at[t, w])
            if t:
                for cp in plane_sends(t):
                    cp.start()
            half_send(t, par).start()
        when(in_plane(t), go)

    def pass_tile(t):
        @pl.when(y != tiles[t][2])
        def _():
            got_piece(t, mpart(t, par * 128, 128), r5.at[t])
            half_send(t, par).start()

    def half_got(t):
        half_send(t, 1 - par).wait_recv()

    s = 1 - 2 * par

    def scatter(c):
        pp, qq = scatter_to(c)
        return send(at.at[c], bulk.at[qq], ss.at[c], rt.at[0], pp, qq)

    def arrive():
        return send(bulk.at[q], bulk.at[q], ss.at[0], rt.at[0], from_p, from_q)

    def part(t, lo, n):
        return bulk.at[t, pl.ds(lo, n), :]

    def hop(t, lo, n, ssem, rsem, to):
        return send(part(t, lo, n), part(t, lo, n), ssem, rsem, p, to)

    def az(n, way):
        w = s * way
        t = zat(-n * w)
        return hop(t, 0, HA, saz.at[n if way > 0 else 4 + n], ra.at[t], zat(w))

    def bz(dx, n, way):
        w = s * way
        t = 8 * lax.rem(x + dx + 4, 4) + lax.rem(z - n * w + 16, 8)
        return hop(t, HA, HB, sbz.at[dx % 4, n if way > 0 else 4 + n], rb.at[t], zat(w))

    def ax(dz, way):
        t = zat(dz)
        return hop(t, 0, HA, sax.at[dz % 8, 0 if way > 0 else 1], ra.at[t], xat(way))

    def axf(dz, way):
        zz = lax.rem(z + dz + 16, 8)
        t = 8 * lax.rem(x - way + 4, 4) + zz
        h = 0 if way > 0 else 1
        return hop(t, h * (HA // 2), HA // 2, sax.at[dz % 8, 2 + h], rah.at[zz, h], xat(way))

    def bx(n):
        return hop(q, HA, HB, sbx.at[n], rb.at[q], xat(n + 1))

    def got(t, lo, n, rsem):
        hop(t, lo, n, saz.at[0], rsem, xat(1)).wait_recv()

    def got_a(t):
        got(t, 0, HA, ra.at[t])

    def got_b(t):
        got(t, HA, HB, rb.at[t])

    def last(way):
        return 4 if way > 0 else 3

    def start_event():
        @pl.when(from_self)
        def _():
            cp = pltpu.make_async_copy(at.at[0], bulk.at[q], rt.at[0])
            cp.start()
            cp.wait()

        @pl.when(jnp.logical_not(from_self))
        def _():
            arrive().wait_recv()
        for n in (0, 2, 1):
            bx(n).start()
        for way in (1, -1):
            az(0, way).start()
            bz(0, 0, way).start()
        for way in (1, -1):
            ax(0, way).start()

    def az_event(n):
        for way in (1, -1):
            if n <= last(way):
                got_a(zat(-n * s * way))
                if n < last(way):
                    az(n, way).start()
        for dz in ((n, -n) if n < 4 else (4,)):
            for way in (1, -1):
                ax(dz, way).start()

    def bx_event():
        for dx in (1, -1, 2):
            got_b(xat(dx))
            for way in (1, -1):
                bz(dx, 0, way).start()

    def bz_event(dx, n):
        for way in (1, -1):
            if n <= last(way):
                got_b(8 * lax.rem(x + dx + 4, 4) + lax.rem(z - n * s * way + 16, 8))
                if n < last(way):
                    bz(dx, n, way).start()

    def ax_event(dz):
        zz = lax.rem(z + dz + 16, 8)
        for way in (1, -1):
            got_a(8 * lax.rem(x - way + 4, 4) + zz)
            axf(dz, way).start()

    def ax2_event(dz):
        zz = lax.rem(z + dz + 16, 8)
        t = 8 * lax.rem(x + 2, 4) + zz
        for h in range(2):
            got(t, h * (HA // 2), HA // 2, rah.at[zz, h])

    E = functools.partial
    xs = (0, 1, -1, 2)
    def strips_event():
        @pl.when(p < NP)
        def _():
            for c in range(2):
                for cp in origin(c):
                    cp.start()
                g_ref[tile(p), c * B:(c + 1) * B] = a_ref[c]

    events = {
        (0, 0): [E(half_tile, t) for t in (1, 2, 3, 4)],
        (0, 1): [start_event],
        (0, 2): [E(half_tile, t) for t in (5, 6, 7, 8, 9)],
        (0, 5): [E(pass_tile, t) for t in (1, 2, 3, 4)],
        (0, 6): [E(az_event, 1), strips_event],
        (0, 7): [bx_event, E(bz_event, 0, 1)],
        (1, 0): [E(pass_tile, t) for t in (5, 6, 7, 8, 9)] + [E(ax_event, 0)],
        (1, 3): [E(az_event, 2)],
        (1, 4): [E(bz_event, dx, 1) for dx in (1, -1, 2)],
        (1, 5): [E(bz_event, 0, 2)],
        (1, 6): [E(ax_event, 1), E(ax_event, -1)],
        (1, 7): [E(relay_event, i, c, False) for c in range(2) for i in range(2)],
        (2, 0): [E(az_event, 3)],
        (2, 1): [E(bz_event, dx, 2) for dx in (1, -1, 2)],
        (2, 2): [E(ax_event, 2), E(ax_event, -2)],
        (2, 3): [E(bz_event, 0, 3)],
        (2, 5): [E(relay_event, i, c, True) for c in range(2) for i in range(2)],
        (2, 7): [E(az_event, 4)],
        (3, 0): [E(bz_event, dx, 3) for dx in (1, -1, 2)],
        (3, 1): [E(ax_event, 3), E(ax_event, -3)],
        (3, 6): [E(ax_event, 4)],
    }

    def scatter_start():
        at[0] = a_ref[0].T
        at[1] = a_ref[1].T
        for c in range(2):
            pl.when(jnp.logical_not(scatter_self(c)))(scatter(c).start)

    @pl.when(origin_dev)
    def _():
        each_piece(lambda cp: cp.start())

        @pl.when(plane == y)
        def _():
            lo = pl.multiple_of(my_lo, 16)
            m_ref[pl.ds(pl.multiple_of(p * B + my_lo, 16), 16), tile(q)] = a_ref[0, pl.ds(lo, 16), :]
    pl.when((p < NP) & (x != 0))(scatter_start)
    relay_tile(0)
    pl.when((p < NP) & (x == 0))(scatter_start)
    for t in range(1, 10):
        relay_tile(t)
    ring_tile(0)
    for t in range(1, 10):
        ring_tile(t)
    S[...] = jnp.zeros_like(S)
    half_tile(0)

    row = lax.broadcasted_iota(jnp.int32, (B, B), 0)
    col = lax.broadcasted_iota(jnp.int32, (B, B), 1)

    def step(k, _):
        for t, (kk, kc, _) in enumerate(tiles):
            if kk == kc:
                pl.when(k == kk)(functools.partial(half_got, t))

        T[...] = S[tile(k), tile(k)] + m_ref[tile(k), tile(k)]

        def between(jb):
            for kk in range(NP):
                for ev in events.get((kk, jb), ()):
                    pl.when(k == kk)(ev)

        factor_tile(T, between)
        S[tile(k), tile(k)] = T[...]
        X = jnp.where(row >= col, T[...], 0.0)
        for t, (kk, kc, _) in enumerate(tiles):
            if kk != kc:
                pl.when(k == kk)(functools.partial(half_got, t))

        def solve(m, _):
            S[tile(k), tile(m)] = dot3(X, S[tile(k), tile(m)] + m_ref[tile(k), tile(m)])
            return 0

        lax.fori_loop(k + 1, NP, solve, 0)

        def trail(i, _):
            left = S[tile(k), tile(i)].T

            def inner(m, _):
                S[tile(i), tile(m)] = S[tile(i), tile(m)] - dot3(left, S[tile(k), tile(m)])
                return 0

            lax.fori_loop(i, NP, inner, 0)
            return 0

        lax.fori_loop(k + 1, NP, trail, 0)
        return 0

    lax.fori_loop(0, NP, step, 0)

    for i in range(2):
        for c in range(2):
            relay(1 - par + 2 * i, c).wait_recv()

    def block(i, j):
        return S[i * B:(i + 1) * B, j * B:(j + 1) * B]

    for k in range(NP):
        acc = g_ref[k * B:(k + 1) * B, :]
        for i in range(k):
            acc = acc - dot3(block(i, k).T, W[i * B:(i + 1) * B, :])
        W[k * B:(k + 1) * B, :] = dot3(jnp.where(row >= col, block(k, k), 0.0), acc)

    kq = jnp.minimum(q, NP - 1)
    kp = jnp.minimum(p, NP - 1)
    u = S[tile(kq), tile(kp)]
    u_diag = jnp.where(col > row, u, jnp.where(col == row, 1.0 / u, 0.0))
    u = jnp.where(kp == kq, u_diag, jnp.where(kq < kp, u, 0.0))
    l_ref[...] = u.T

    col2 = lax.broadcasted_iota(jnp.int32, (B, 2 * B), 1)
    row2 = lax.broadcasted_iota(jnp.int32, (B, 2 * B), 0)
    for k in (3, 2, 1, 0):
        unit = jnp.where((row2 == col2) & (q == k), 1.0, 0.0)
        acc = jnp.where((col2 < B) & (q < NP), unit, W[k * B:(k + 1) * B, :])
        for m in range(k + 1, NP):
            acc = acc - dot3(S[k * B:(k + 1) * B, m * B:(m + 1) * B], W[m * B:(m + 1) * B, :])
        X = jnp.where(row >= col, S[k * B:(k + 1) * B, k * B:(k + 1) * B], 0.0)
        w = dot3(X.T, acc)
        W[k * B:(k + 1) * B, :] = w
        hi, lo = split(w)
        whi_ref[k * B:(k + 1) * B, :] = hi
        wlo_ref[k * B:(k + 1) * B, :] = lo

    for dx in xs:
        bz_event(dx, 4)
    for dz in range(8):
        ax2_event(dz)

    @pl.when(p < NP)
    def _():
        for c in range(2):
            for cp in origin(c):
                cp.wait_send()
            pl.when(jnp.logical_not(scatter_self(c)))(scatter(c).wait_send)
    for c in range(2):
        for i in range(2):
            k = par + 2 * i
            pl.when(k != p)(relay(k, c).wait_send)
            cond, cp = onward(i, c)
            pl.when(cond)(cp.wait_send)
    pl.when(origin_dev)(lambda: each_piece(lambda cp: cp.wait_send()))
    for t in range(10):
        @pl.when((x == 0) & (y == tiles[t][2]))
        def _():
            for cp in relay_sends(t):
                cp.wait_send()

        def drain():
            for d in range(1, 8):
                ring_send(t, d).wait_send()
            if t:
                for cp in plane_sends(t):
                    cp.wait_send()
        when(in_plane(t), drain)
        half_send(t, par).wait_send()
    for n in range(3):
        bx(n).wait_send()
    for way in (1, -1):
        for n in range(last(way)):
            az(n, way).wait_send()
            for dx in xs:
                bz(dx, n, way).wait_send()
        for dz in range(8):
            ax(dz, way).wait_send()
            axf(dz, way).wait_send()


def main(a):
    dma = pltpu.SemaphoreType.DMA
    vmem = pl.BlockSpec(memory_space=pltpu.VMEM)
    return pl.pallas_call(
        main_kernel,
        out_shape=(
            jax.ShapeDtypeStruct((32, B, B), F32),
            jax.ShapeDtypeStruct((TOP, 2 * B), BF16),
            jax.ShapeDtypeStruct((TOP, 2 * B), BF16),
            jax.ShapeDtypeStruct((B, B), F32),
        ),
        in_specs=[vmem],
        out_specs=[vmem] * 4,
        scratch_shapes=[
            pltpu.VMEM((2, B, B), F32),
            pltpu.VMEM((TOP, TOP), F32),
            pltpu.VMEM((TOP, 2 * B), F32),
            pltpu.VMEM((TOP, TOP), F32),
            pltpu.VMEM((B, B), F32),
            pltpu.VMEM((TOP, 2 * B), F32),
            dma((NP, 2)), dma((2, 3)), dma((NP, 2)), dma((2, 2)),
            dma((10,)), dma((10,)), dma((10, 8)), dma((10,)), dma((10,)),
            dma((2, 8)), dma((16,)), dma((10, 3)), dma((10, 8)), dma((10,)), dma((10, 3)),
            dma((1,)), dma((2,)), dma((32,)), dma((8, 2)), dma((32,)),
            dma((7,)), dma((8, 4)), dma((3,)), dma((4, 7)),
        ],
        compiler_params=pltpu.CompilerParams(
            collective_id=1, has_side_effects=True, vmem_limit_bytes=30 * 1024 * 1024),
        cost_estimate=pl.CostEstimate(
            flops=60_000_000_000, bytes_accessed=8_000_000, transcendentals=0),
        name="main",
    )(a)


def update_kernel(p_ref, b0, b1, b2, b3, m_ref, whi_ref, wlo_ref, l_ref, o_ref):
    r = pl.program_id(0)
    p = p_ref[0]
    q = p_ref[1]
    acc = jnp.zeros((B, 2 * B), F32)
    for k, b_ref in enumerate((b0, b1, b2, b3)):
        left = b_ref[0].astype(BF16)
        acc = acc + dot1(left, whi_ref[k * B:(k + 1) * B, :])
        acc = acc + dot1(left, wlo_ref[k * B:(k + 1) * B, :])
    m = m_ref[0].astype(F32)
    top = (r == 0) & (p < NP)
    factor_col = q < NP
    c0 = jnp.where(factor_col, acc[:, 0:B], m[:, 0:B] - acc[:, 0:B])
    c0 = jnp.where(top, jnp.where(factor_col, l_ref[...], 0.0), c0)
    c1 = jnp.where(top, 0.0, m[:, B:] - acc[:, B:])
    for n, part in enumerate((c0[:, :128], c0[:, 128:], c1[:, :128], c1[:, 128:])):
        o_ref[pl.ds(n, B, stride=4), :] = part


def update(place, bulk, mine, whi, wlo, ltile):
    def stream(k):
        def index(r, place):
            return 8 * (r % 4) + (place[0] + 4 * (r // 4) + k) % 8, 0, 0
        return pl.BlockSpec((1, B, B), index)

    return pl.pallas_call(
        update_kernel,
        out_shape=jax.ShapeDtypeStruct((8 * 4 * B, 128), F32),
        grid_spec=pltpu.PrefetchScalarGridSpec(
            num_scalar_prefetch=1,
            grid=(8,),
            in_specs=[stream(k) for k in range(NP)] + [
                pl.BlockSpec((1, B, 2 * B), lambda r, place: (r, 0, 0)),
                pl.BlockSpec((TOP, 2 * B), lambda r, place: (0, 0)),
                pl.BlockSpec((TOP, 2 * B), lambda r, place: (0, 0)),
                pl.BlockSpec((B, B), lambda r, place: (0, 0)),
            ],
            out_specs=pl.BlockSpec((4 * B, 128), lambda r, place: (r, 0)),
        ),
        compiler_params=pltpu.CompilerParams(vmem_limit_bytes=20 * 1024 * 1024),
        cost_estimate=pl.CostEstimate(
            flops=4_300_000_000, bytes_accessed=16_000_000, transcendentals=0),
        name="update",
    )(place, bulk, bulk, bulk, bulk, mine, whi, wlo, ltile)


def local(covariance):
    mine = covariance.reshape(8, B, 2, B)
    a = mine[0].astype(F32).transpose(1, 0, 2)
    mine = mine.reshape(8, B, 2 * B)
    bulk, whi, wlo, ltile = main(a)
    place = jnp.stack([lax.axis_index("prow"), lax.axis_index("pcol")]).astype(jnp.int32)
    out = update(place, bulk, mine, whi, wlo, ltile)
    return out.reshape(8, 1, B, 2, 1, B)


def solution(mesh):
    in_specs = (P(None, "prow", None, None, "pcol", None),)
    out_specs = P(None, "prow", None, None, "pcol", None)
    return jax.shard_map(local, mesh=mesh, in_specs=in_specs, out_specs=out_specs, check_vma=False)
```

```python
import functools
import jax
import jax.numpy as jnp
from jax import lax
from jax.experimental import pallas as pl
from jax.experimental.pallas import tpu as pltpu
from jax.sharding import PartitionSpec as P

B = 256
NP = 4
TOP = NP * B
F32 = jnp.float32
BF16 = jnp.bfloat16
MESH = pl.DeviceIdType.MESH


def split(a):
    hi = a.astype(BF16)
    return hi, (a - hi.astype(F32)).astype(BF16)


def dot1(a, b):
    return jnp.dot(a, b, preferred_element_type=F32)


def dot3(a, b):
    ah, al = split(a)
    bh, bl = split(b)
    return dot1(ah, bh) + (dot1(ah, bl) + dot1(al, bh))


def panel(R, j, sub, lane):
    for g in range(4):
        c0 = j + 8 * g
        lt = c0 // 128
        o = c0 % 128
        cb = {}
        for h in range(g, 4):
            for t in range(8):
                cb[h, t] = jnp.broadcast_to(R[h][lt][:, o + t:o + t + 1], (8, 128))
        inblk = (lane >= o) & (lane < o + 8)
        R[g][lt] = jnp.where(inblk, jnp.where(lane - o == sub, 1.0, 0.0), R[g][lt])
        for h in range(g + 1, 4):
            R[h][lt] = jnp.where(inblk, 0.0, R[h][lt])
        scale = jnp.zeros((8, 128), F32)
        for t in range(8):
            piv = jnp.broadcast_to(cb[g, t][t:t + 1, :], (8, 128))
            inv = 1.0 / piv
            scale = jnp.where(sub == t, lax.rsqrt(piv), scale)
            rows = [jnp.broadcast_to(R[g][l][t:t + 1, :], (8, 128)) for l in range(2)]
            crow = {u: jnp.broadcast_to(cb[g, u][t:t + 1, :], (8, 128)) for u in range(t + 1, 8)}
            for h in range(g, 4):
                f = cb[h, t] * inv
                if h == g:
                    f = jnp.where(sub > t, f, 0.0)
                for l in range(2):
                    R[h][l] = R[h][l] - f * rows[l]
                for u in range(t + 1, 8):
                    cb[h, u] = cb[h, u] - f * crow[u]
        for u in range(1, 8):
            R[g][lt] = jnp.where((lane == o + u) & (sub < u), cb[g, u], R[g][lt])
        for l in range(2):
            R[g][l] = R[g][l] * scale
    return R


def factor_tile(T, between):
    sub = lax.broadcasted_iota(jnp.int32, (8, 128), 0)
    lane = lax.broadcasted_iota(jnp.int32, (8, 128), 1)
    pr = lax.broadcasted_iota(jnp.int32, (32, B), 0)
    pc = lax.broadcasted_iota(jnp.int32, (32, B), 1)
    for jb in range(8):
        between(jb)
        j = 32 * jb
        R = [[T[j + 8 * g:j + 8 * g + 8, 128 * l:128 * l + 128] for l in range(2)] for g in range(4)]
        R = panel(R, j, sub, lane)
        rows = jnp.concatenate([jnp.concatenate(r, axis=1) for r in R], axis=0)
        T[j:j + 32, :] = rows
        if jb < 7:
            left = rows.T[j + 32:, :]
            n = B - j - 32
            ln = lax.broadcasted_iota(jnp.int32, (n, B), 1)
            low = jnp.where((ln >= j) & (ln < j + 32), 0.0, T[j + 32:, :])
            rows = jnp.where((pc < j + 32) & (pc > j + pr), 0.0, rows)
            T[j + 32:, :] = low - dot3(left, rows)


HA = 160
HB = B - HA


def main_kernel(a_ref, bulk, whi_ref, wlo_ref, l_ref,
                at, m_ref, g_ref, S, T, W,
                rg, so, sf, sg, r1, r2, r3, r4, r5, s1, s2, s2b, s3, s4, s5,
                rt, ss, ra, rah, rb, rbx, saz, sax, sbx, sbz):
    p = lax.axis_index("prow")
    q = lax.axis_index("pcol")
    x = q // 8
    z = q % 8
    par = p % 2
    sib = p + 1 - 2 * par

    def zat(d):
        return 8 * x + lax.rem(z + d + 16, 8)

    def xat(d):
        return lax.rem(q + 8 * d + 64, 32)

    barrier = pltpu.get_barrier_semaphore()

    def greet(pp, qq):
        pl.semaphore_signal(barrier, inc=1, device_id=(pp, qq), device_id_type=MESH)

    y = p // 2
    for d in range(1, 8):
        greet(lax.rem(p + d, 8), q)
        greet(p, zat(d))
    for d in (1, 2, 3):
        greet(p, xat(d))
    count = jnp.int32(17)

    from_p, from_q = lax.rem(z - p + 8, 4), 8 * x + p
    from_self = (p == 0) & (z == 0)

    def scatter_to(c):
        return z, 8 * x + lax.rem(z + 4 * c + p, 8)

    def scatter_self(c):
        return (p == 0) & (z == 0) & (c == 0)

    def greet_if(cond, pp, qq):
        pl.when(cond)(functools.partial(greet, pp, qq))
        return jnp.where(cond, 1, 0)

    count = count + greet_if(jnp.logical_not(from_self), from_p, from_q)
    for c in range(2):
        count = count + greet_if((p < NP) & jnp.logical_not(scatter_self(c)), *scatter_to(c))

    tiles = ((0, 0, 0), (0, 1, 0), (0, 2, 1), (0, 3, 2), (1, 1, 3),
             (1, 2, 0), (1, 3, 1), (2, 2, 2), (2, 3, 3), (3, 3, 0))
    origin_dev = (p < NP) & (p <= q) & (q < NP)
    plane = jnp.int32(0)
    my_tile = jnp.int32(0)
    for t, (k, kc, yt) in enumerate(tiles):
        me = (p == k) & (q == kc)
        plane = jnp.where(me, yt, plane)
        my_tile = jnp.where(me, t, my_tile)
        count = count + greet_if((x == 0) & (y == yt) & jnp.logical_not(me), k, kc)

    def piece_targets():
        for c in range(2):
            for d in range(8):
                yield c, d, (2 * plane + c), lax.rem(z + d, 8)

    for c, d, pp, qq in piece_targets():
        cond = origin_dev & jnp.logical_not((p == pp) & (q == qq))
        count = count + greet_if(cond, pp, qq)
    relay0 = (x == 0) & (y == 0)
    count = count + greet_if(jnp.logical_not(relay0), par, z)

    def relay_targets():
        for dy in range(4):
            for dx in range(4):
                if dx or dy:
                    yield 4 * dy + dx, 2 * lax.rem(y + dy, 4) + par, xat(dx)

    for _, pp, qq in relay_targets():
        count = count + greet_if(relay0, pp, qq)
    pl.semaphore_wait(barrier, count)

    def send(src, dst, ssem, rsem, pp, qq):
        return pltpu.make_async_remote_copy(
            src_ref=src, dst_ref=dst, send_sem=ssem, recv_sem=rsem,
            device_id=(pp, qq), device_id_type=MESH,
        )

    def tile(i):
        return pl.ds(pl.multiple_of(i * B, B), B)

    def gslot(k, c):
        return g_ref.at[tile(k), pl.ds(c * B, B)]

    def origin(c):
        for n, d in enumerate((2, 6, None)):
            pp = sib if d is None else lax.rem(p + d, 8)
            yield send(a_ref.at[c], gslot(p, c), so.at[c, n], rg.at[p, c], pp, q)

    def relay(k, c):
        return send(gslot(k, c), gslot(k, c), sf.at[k, c], rg.at[k, c], sib, q)

    def onward(i, c):
        k = par + 2 * i
        pp = lax.rem(p + (2 if c == 0 else 6), 8)
        return y == (i + (1 if c == 0 else 3)) % 4, send(
            gslot(k, c), gslot(k, c), sg.at[i, c], rg.at[k, c], pp, q)

    def relay_event(i, c, far):
        k = par + 2 * i
        opposite = y == (i + 2) % 4

        @pl.when(opposite if far else (k != p) & jnp.logical_not(opposite))
        def _():
            relay(k, c).wait_recv()
            relay(k, c).start()
            if not far:
                cond, cp = onward(i, c)
                pl.when(cond)(cp.start)

    def mpart(t, lo, n):
        k, kc, _ = tiles[t]
        return m_ref.at[pl.ds(pl.multiple_of(k * B + lo, 16), n), pl.ds(kc * B, B)]

    def one_piece(c, d, pp, qq):
        lo = pl.multiple_of(c * 128 + 16 * qq, 16)
        dst = m_ref.at[pl.ds(pl.multiple_of(p * B + c * 128 + 16 * qq, 16), 16), tile(q)]
        return send(a_ref.at[0, pl.ds(lo, 16), :], dst, s1.at[c, d], r1.at[my_tile], pp, qq)

    def each_piece(act):
        for c, d, pp, qq in piece_targets():
            cp = one_piece(c, d, pp, qq)
            if d == 0:
                pl.when((p != pp))(functools.partial(act, cp))
            else:
                act(cp)

    my_lo = par * 128 + 16 * z

    def my_piece(t):
        return mpart(t, my_lo, 16)

    def got_piece(t, ref, rsem):
        send(ref, ref, s1.at[0, 0], rsem, sib, q).wait_recv()

    def relay_sends(t):
        if t == 0:
            for n, pp, qq in relay_targets():
                yield send(my_piece(t), my_piece(t), s2.at[n], r2.at[t], pp, qq)
        else:
            for n in range(3):
                yield send(my_piece(t), my_piece(t), s2b.at[t, n], r2.at[t], p, xat(n + 1))

    def relay_tile(t):
        k, kc, yt = tiles[t]

        @pl.when((x == 0) & (y == yt))
        def _():
            @pl.when(jnp.logical_not((p == k) & (q == kc)))
            def _():
                got_piece(t, my_piece(t), r1.at[t])
            for cp in relay_sends(t):
                cp.start()

    def in_plane(t):
        return None if t == 0 else y == tiles[t][2]

    def when(cond, f):
        if cond is None:
            f()
        else:
            pl.when(cond)(f)

    def ring_send(t, d):
        return send(my_piece(t), my_piece(t), s3.at[t, d], r3.at[t, z], p, zat(d))

    def ring_tile(t):
        def go():
            @pl.when(jnp.logical_not((x == 0) & (y == tiles[t][2])))
            def _():
                got_piece(t, my_piece(t), r2.at[t])
            for d in (4, 3, 5, 2, 6, 1, 7):
                ring_send(t, d).start()
        when(in_plane(t), go)

    def half_send(t, c):
        part = mpart(t, c * 128, 128)
        return send(part, part, s4.at[t], r4.at[t], sib, q)

    def plane_sends(t):
        part = mpart(t, par * 128, 128)
        for n in range(3):
            yield send(part, part, s5.at[t, n], r5.at[t], lax.rem(p + 2 * n + 2, 8), q)

    def half_tile(t):
        def go():
            for d in range(1, 8):
                w = lax.rem(z + d, 8)
                got_piece(t, mpart(t, par * 128 + 16 * w, 16), r3.at[t, w])
            if t:
                for cp in plane_sends(t):
                    cp.start()
            half_send(t, par).start()
        when(in_plane(t), go)

    def pass_tile(t):
        @pl.when(y != tiles[t][2])
        def _():
            got_piece(t, mpart(t, par * 128, 128), r5.at[t])
            half_send(t, par).start()

    def half_got(t):
        half_send(t, 1 - par).wait_recv()

    s = 1 - 2 * par

    def xm(d):
        return lax.rem(x + d + 4, 4)

    def zm(d):
        return lax.rem(z + d + 16, 8)

    def scatter(c, b):
        pp, qq = scatter_to(c)
        rows = pl.ds(HA, HB) if b else pl.ds(0, HA)
        return send(at.at[c, rows, :], bulk.at[lax.rem(z + 4 * c + p, 8), x, rows, :],
                    ss.at[c, b], rt.at[b], pp, qq)

    def hop(ref, ssem, rsem, to):
        return send(ref, ref, ssem, rsem, p, to)

    def got(ref, rsem):
        hop(ref, saz.at[0], rsem, xat(1)).wait_recv()

    def part_a(zz, xx):
        return bulk.at[zz, xx, pl.ds(0, HA), :]

    def half_a(zz, xx, h):
        return bulk.at[zz, xx, pl.ds(h * (HA // 2), HA // 2), :]

    def part_b(zz, xx):
        return bulk.at[zz, xx, pl.ds(HA, HB), :]

    def row_b(zz):
        return bulk.at[zz, :, pl.ds(HA, HB), :]

    def az(n, way):
        w = s * way
        zz = zm(-n * w)
        return hop(part_a(zz, x), saz.at[n if way > 0 else 4 + n], ra.at[zz, x], zat(w))

    def bz(n, way):
        w = s * way
        zz = zm(-n * w)
        return hop(row_b(zz), sbz.at[n if way > 0 else 4 + n], rb.at[zz], zat(w))

    def ax(dz, way):
        zz = zm(dz)
        return hop(part_a(zz, x), sax.at[dz % 8, 0 if way > 0 else 1], ra.at[zz, x], xat(way))

    def axf(dz, way):
        zz = zm(dz)
        h = 0 if way > 0 else 1
        return hop(half_a(zz, xm(-way), h), sax.at[dz % 8, 2 + h], rah.at[zz, h], xat(way))

    def bx(n):
        return hop(part_b(z, x), sbx.at[n], rbx.at[x], xat(n + 1))

    def last(way):
        return 4 if way > 0 else 3

    def arrive(b):
        rows = pl.ds(HA, HB) if b else pl.ds(0, HA)
        own = bulk.at[z, x, rows, :]

        @pl.when(from_self)
        def _():
            cp = pltpu.make_async_copy(at.at[0, rows, :], own, rt.at[b])
            cp.start()
            cp.wait()

        @pl.when(jnp.logical_not(from_self))
        def _():
            send(own, own, ss.at[0, b], rt.at[b], from_p, from_q).wait_recv()

    def start_b_event():
        arrive(1)
        for n in (0, 2, 1):
            bx(n).start()

    def start_event():
        arrive(0)
        for way in (1, -1):
            az(0, way).start()
        for way in (1, -1):
            ax(0, way).start()

    def az_event(n):
        for way in (1, -1):
            if n <= last(way):
                zz = zm(-n * s * way)
                got(part_a(zz, x), ra.at[zz, x])
                if n < last(way):
                    az(n, way).start()
        for dz in ((n, -n) if n < 4 else (4,)):
            for way in (1, -1):
                ax(dz, way).start()

    def bx_event():
        for dx in (1, -1, 2):
            got(part_b(z, xm(dx)), rbx.at[xm(dx)])
        for way in (1, -1):
            bz(0, way).start()

    def bz_event(n):
        for way in (1, -1):
            if n <= last(way):
                zz = zm(-n * s * way)
                got(row_b(zz), rb.at[zz])
                if n < last(way):
                    bz(n, way).start()

    def ax_event(dz):
        zz = zm(dz)
        for way in (1, -1):
            got(part_a(zz, xm(-way)), ra.at[zz, xm(-way)])
            axf(dz, way).start()

    def ax2_event(dz):
        zz = zm(dz)
        for h in range(2):
            got(half_a(zz, xm(2), h), rah.at[zz, h])

    E = functools.partial
    def strips_event():
        @pl.when(p < NP)
        def _():
            for c in range(2):
                for cp in origin(c):
                    cp.start()
                g_ref[tile(p), c * B:(c + 1) * B] = a_ref[c]

    events = {
        (0, 0): [E(half_tile, t) for t in (1, 2, 3, 4)],
        (0, 2): [E(half_tile, t) for t in (5, 6, 7, 8, 9)],
        (0, 5): [E(pass_tile, t) for t in (1, 2, 3, 4)],
        (0, 6): [strips_event],
        (0, 7): [E(az_event, 1)],
        (1, 0): [E(pass_tile, t) for t in (5, 6, 7, 8, 9)] + [E(bz_event, 1)],
        (1, 4): [E(ax_event, 0)],
        (1, 5): [E(az_event, 2)],
        (1, 7): [E(relay_event, i, c, False) for c in range(2) for i in range(2)],
        (2, 0): [E(bz_event, 2), E(ax_event, 1), E(ax_event, -1)],
        (2, 3): [E(az_event, 3)],
        (2, 5): [E(relay_event, i, c, True) for c in range(2) for i in range(2)],
        (2, 6): [E(ax_event, 2), E(ax_event, -2)],
        (3, 0): [E(bz_event, 3)],
        (3, 1): [E(az_event, 4)],
        (3, 3): [E(ax_event, 3), E(ax_event, -3)],
        (3, 7): [E(ax_event, 4)],
    }

    def scatter_start():
        at[0] = a_ref[0].T
        at[1] = a_ref[1].T
        for b in (1, 0):
            for c in range(2):
                pl.when(jnp.logical_not(scatter_self(c)))(scatter(c, b).start)

    @pl.when(origin_dev)
    def _():
        each_piece(lambda cp: cp.start())

        @pl.when(plane == y)
        def _():
            lo = pl.multiple_of(my_lo, 16)
            m_ref[pl.ds(pl.multiple_of(p * B + my_lo, 16), 16), tile(q)] = a_ref[0, pl.ds(lo, 16), :]
    pl.when(p < NP)(scatter_start)
    relay_tile(0)
    ring_tile(0)
    for t in range(1, 10):
        relay_tile(t)
    S[...] = jnp.zeros_like(S)
    start_b_event()
    half_tile(0)
    for t in range(1, 10):
        ring_tile(t)
    start_event()
    bx_event()

    row = lax.broadcasted_iota(jnp.int32, (B, B), 0)
    col = lax.broadcasted_iota(jnp.int32, (B, B), 1)

    def step(k, _):
        for t, (kk, kc, _) in enumerate(tiles):
            if kk == kc:
                pl.when(k == kk)(functools.partial(half_got, t))

        T[...] = S[tile(k), tile(k)] + m_ref[tile(k), tile(k)]

        def between(jb):
            for kk in range(NP):
                for ev in events.get((kk, jb), ()):
                    pl.when(k == kk)(ev)

        factor_tile(T, between)
        S[tile(k), tile(k)] = T[...]
        X = jnp.where(row >= col, T[...], 0.0)
        for t, (kk, kc, _) in enumerate(tiles):
            if kk != kc:
                pl.when(k == kk)(functools.partial(half_got, t))

        def solve(m, _):
            S[tile(k), tile(m)] = dot3(X, S[tile(k), tile(m)] + m_ref[tile(k), tile(m)])
            return 0

        lax.fori_loop(k + 1, NP, solve, 0)

        def trail(i, _):
            left = S[tile(k), tile(i)].T

            def inner(m, _):
                S[tile(i), tile(m)] = S[tile(i), tile(m)] - dot3(left, S[tile(k), tile(m)])
                return 0

            lax.fori_loop(i, NP, inner, 0)
            return 0

        lax.fori_loop(k + 1, NP, trail, 0)
        return 0

    lax.fori_loop(0, NP, step, 0)

    for i in range(2):
        for c in range(2):
            relay(1 - par + 2 * i, c).wait_recv()

    def block(i, j):
        return S[i * B:(i + 1) * B, j * B:(j + 1) * B]

    for k in range(NP):
        acc = g_ref[k * B:(k + 1) * B, :]
        for i in range(k):
            acc = acc - dot3(block(i, k).T, W[i * B:(i + 1) * B, :])
        W[k * B:(k + 1) * B, :] = dot3(jnp.where(row >= col, block(k, k), 0.0), acc)

    kq = jnp.minimum(q, NP - 1)
    kp = jnp.minimum(p, NP - 1)
    u = S[tile(kq), tile(kp)]
    u_diag = jnp.where(col > row, u, jnp.where(col == row, 1.0 / u, 0.0))
    u = jnp.where(kp == kq, u_diag, jnp.where(kq < kp, u, 0.0))
    l_ref[...] = u.T

    col2 = lax.broadcasted_iota(jnp.int32, (B, 2 * B), 1)
    row2 = lax.broadcasted_iota(jnp.int32, (B, 2 * B), 0)
    for k in (3, 2, 1, 0):
        unit = jnp.where((row2 == col2) & (q == k), 1.0, 0.0)
        acc = jnp.where((col2 < B) & (q < NP), unit, W[k * B:(k + 1) * B, :])
        for m in range(k + 1, NP):
            acc = acc - dot3(S[k * B:(k + 1) * B, m * B:(m + 1) * B], W[m * B:(m + 1) * B, :])
        X = jnp.where(row >= col, S[k * B:(k + 1) * B, k * B:(k + 1) * B], 0.0)
        w = dot3(X.T, acc)
        W[k * B:(k + 1) * B, :] = w
        hi, lo = split(w)
        whi_ref[k * B:(k + 1) * B, :] = hi
        wlo_ref[k * B:(k + 1) * B, :] = lo

    bz_event(4)
    for dz in range(8):
        ax2_event(dz)

    @pl.when(p < NP)
    def _():
        for c in range(2):
            for cp in origin(c):
                cp.wait_send()
            for b in (1, 0):
                pl.when(jnp.logical_not(scatter_self(c)))(scatter(c, b).wait_send)
    for c in range(2):
        for i in range(2):
            k = par + 2 * i
            pl.when(k != p)(relay(k, c).wait_send)
            cond, cp = onward(i, c)
            pl.when(cond)(cp.wait_send)
    pl.when(origin_dev)(lambda: each_piece(lambda cp: cp.wait_send()))
    for t in range(10):
        @pl.when((x == 0) & (y == tiles[t][2]))
        def _():
            for cp in relay_sends(t):
                cp.wait_send()

        def drain():
            for d in range(1, 8):
                ring_send(t, d).wait_send()
            if t:
                for cp in plane_sends(t):
                    cp.wait_send()
        when(in_plane(t), drain)
        half_send(t, par).wait_send()
    for n in range(3):
        bx(n).wait_send()
    for way in (1, -1):
        for n in range(last(way)):
            az(n, way).wait_send()
            bz(n, way).wait_send()
        for dz in range(8):
            ax(dz, way).wait_send()
            axf(dz, way).wait_send()


def main(a):
    dma = pltpu.SemaphoreType.DMA
    vmem = pl.BlockSpec(memory_space=pltpu.VMEM)
    return pl.pallas_call(
        main_kernel,
        out_shape=(
            jax.ShapeDtypeStruct((8, 4, B, B), F32),
            jax.ShapeDtypeStruct((TOP, 2 * B), BF16),
            jax.ShapeDtypeStruct((TOP, 2 * B), BF16),
            jax.ShapeDtypeStruct((B, B), F32),
        ),
        in_specs=[vmem],
        out_specs=[vmem] * 4,
        scratch_shapes=[
            pltpu.VMEM((2, B, B), F32),
            pltpu.VMEM((TOP, TOP), F32),
            pltpu.VMEM((TOP, 2 * B), F32),
            pltpu.VMEM((TOP, TOP), F32),
            pltpu.VMEM((B, B), F32),
            pltpu.VMEM((TOP, 2 * B), F32),
            dma((NP, 2)), dma((2, 3)), dma((NP, 2)), dma((2, 2)),
            dma((10,)), dma((10,)), dma((10, 8)), dma((10,)), dma((10,)),
            dma((2, 8)), dma((16,)), dma((10, 3)), dma((10, 8)), dma((10,)), dma((10, 3)),
            dma((2,)), dma((2, 2)), dma((8, 4)), dma((8, 2)), dma((8,)), dma((4,)),
            dma((7,)), dma((8, 4)), dma((3,)), dma((7,)),
        ],
        compiler_params=pltpu.CompilerParams(
            collective_id=1, has_side_effects=True, vmem_limit_bytes=30 * 1024 * 1024),
        cost_estimate=pl.CostEstimate(
            flops=60_000_000_000, bytes_accessed=8_000_000, transcendentals=0),
        name="main",
    )(a)


def update_kernel(p_ref, b0, b1, b2, b3, m_ref, whi_ref, wlo_ref, l_ref, o_ref):
    r = pl.program_id(0)
    p = p_ref[0]
    q = p_ref[1]
    acc = jnp.zeros((B, 2 * B), F32)
    for k, b_ref in enumerate((b0, b1, b2, b3)):
        left = b_ref[0, 0].astype(BF16)
        acc = acc + dot1(left, whi_ref[k * B:(k + 1) * B, :])
        acc = acc + dot1(left, wlo_ref[k * B:(k + 1) * B, :])
    m = m_ref[...].astype(F32)
    m0 = m[:, 0, :]
    m1 = m[:, 1, :]
    top = (r == 0) & (p < NP)
    factor_col = q < NP
    c0 = jnp.where(factor_col, acc[:, 0:B], m0 - acc[:, 0:B])
    c0 = jnp.where(top, jnp.where(factor_col, l_ref[...], 0.0), c0)
    c1 = jnp.where(top, 0.0, m1 - acc[:, B:])
    for n, part in enumerate((c0[:, :128], c0[:, 128:], c1[:, :128], c1[:, 128:])):
        o_ref[pl.ds(n, B, stride=4), :] = part


def update(place, bulk, mine, whi, wlo, ltile):
    def stream(k):
        def index(r, place):
            return (place[0] + 4 * (r // 4) + k) % 8, r % 4, 0, 0
        return pl.BlockSpec((1, 1, B, B), index)

    return pl.pallas_call(
        update_kernel,
        out_shape=jax.ShapeDtypeStruct((8 * 4 * B, 128), F32),
        grid_spec=pltpu.PrefetchScalarGridSpec(
            num_scalar_prefetch=1,
            grid=(8,),
            in_specs=[stream(k) for k in range(NP)] + [
                pl.BlockSpec((B, 2, B), lambda r, place: (r, 0, 0)),
                pl.BlockSpec((TOP, 2 * B), lambda r, place: (0, 0)),
                pl.BlockSpec((TOP, 2 * B), lambda r, place: (0, 0)),
                pl.BlockSpec((B, B), lambda r, place: (0, 0)),
            ],
            out_specs=pl.BlockSpec((4 * B, 128), lambda r, place: (r, 0)),
        ),
        compiler_params=pltpu.CompilerParams(vmem_limit_bytes=20 * 1024 * 1024),
        cost_estimate=pl.CostEstimate(
            flops=4_300_000_000, bytes_accessed=16_000_000, transcendentals=0),
        name="update",
    )(place, bulk, bulk, bulk, bulk, mine, whi, wlo, ltile)


def local(covariance):
    mine = covariance.reshape(8, B, 2, B)
    a = mine[0].astype(F32).transpose(1, 0, 2)
    mine = mine.reshape(8 * B, 2, B)
    bulk, whi, wlo, ltile = main(a)
    place = jnp.stack([lax.axis_index("prow"), lax.axis_index("pcol")]).astype(jnp.int32)
    out = update(place, bulk, mine, whi, wlo, ltile)
    return out.reshape(8, 1, B, 2, 1, B)


def solution(mesh):
    in_specs = (P(None, "prow", None, None, "pcol", None),)
    out_specs = P(None, "prow", None, None, "pcol", None)
    return jax.shard_map(local, mesh=mesh, in_specs=in_specs, out_specs=out_specs, check_vma=False)
```

```python
import functools
import jax
import jax.numpy as jnp
from jax import lax
from jax.experimental import pallas as pl
from jax.experimental.pallas import tpu as pltpu
from jax.sharding import PartitionSpec as P

B = 256
NP = 4
TOP = NP * B
F32 = jnp.float32
BF16 = jnp.bfloat16
MESH = pl.DeviceIdType.MESH


def split(a):
    hi = a.astype(BF16)
    return hi, (a - hi.astype(F32)).astype(BF16)


def dot1(a, b):
    return jnp.dot(a, b, preferred_element_type=F32)


def dot3(a, b):
    ah, al = split(a)
    bh, bl = split(b)
    return dot1(ah, bh) + (dot1(ah, bl) + dot1(al, bh))


def panel(R, j, sub, lane):
    for g in range(4):
        c0 = j + 8 * g
        lt = c0 // 128
        o = c0 % 128
        cb = {}
        for h in range(g, 4):
            for t in range(8):
                cb[h, t] = jnp.broadcast_to(R[h][lt][:, o + t:o + t + 1], (8, 128))
        inblk = (lane >= o) & (lane < o + 8)
        R[g][lt] = jnp.where(inblk, jnp.where(lane - o == sub, 1.0, 0.0), R[g][lt])
        for h in range(g + 1, 4):
            R[h][lt] = jnp.where(inblk, 0.0, R[h][lt])
        scale = jnp.zeros((8, 128), F32)
        for t in range(8):
            piv = jnp.broadcast_to(cb[g, t][t:t + 1, :], (8, 128))
            inv = 1.0 / piv
            scale = jnp.where(sub == t, lax.rsqrt(piv), scale)
            rows = [jnp.broadcast_to(R[g][l][t:t + 1, :], (8, 128)) for l in range(2)]
            crow = {u: jnp.broadcast_to(cb[g, u][t:t + 1, :], (8, 128)) for u in range(t + 1, 8)}
            for h in range(g, 4):
                f = cb[h, t] * inv
                if h == g:
                    f = jnp.where(sub > t, f, 0.0)
                for l in range(2):
                    R[h][l] = R[h][l] - f * rows[l]
                for u in range(t + 1, 8):
                    cb[h, u] = cb[h, u] - f * crow[u]
        for u in range(1, 8):
            R[g][lt] = jnp.where((lane == o + u) & (sub < u), cb[g, u], R[g][lt])
        for l in range(2):
            R[g][l] = R[g][l] * scale
    return R


def factor_tile(T, between):
    sub = lax.broadcasted_iota(jnp.int32, (8, 128), 0)
    lane = lax.broadcasted_iota(jnp.int32, (8, 128), 1)
    pr = lax.broadcasted_iota(jnp.int32, (32, B), 0)
    pc = lax.broadcasted_iota(jnp.int32, (32, B), 1)
    for jb in range(8):
        between(jb)
        j = 32 * jb
        R = [[T[j + 8 * g:j + 8 * g + 8, 128 * l:128 * l + 128] for l in range(2)] for g in range(4)]
        R = panel(R, j, sub, lane)
        rows = jnp.concatenate([jnp.concatenate(r, axis=1) for r in R], axis=0)
        T[j:j + 32, :] = rows
        if jb < 7:
            left = rows.T[j + 32:, :]
            n = B - j - 32
            ln = lax.broadcasted_iota(jnp.int32, (n, B), 1)
            low = jnp.where((ln >= j) & (ln < j + 32), 0.0, T[j + 32:, :])
            rows = jnp.where((pc < j + 32) & (pc > j + pr), 0.0, rows)
            T[j + 32:, :] = low - dot3(left, rows)


HA = 160
HB = B - HA


def main_kernel(a_ref, bulk, whi_ref, wlo_ref, l_ref,
                at, m_ref, g_ref, S, T, W,
                rg, so, sf, sg, r1, r2, r3, r4, r5, s1, s2, s2b, s3, s4, s5,
                rt, ss, ra, rah, rb, rbx, saz, sax, sbx, sbz):
    p = lax.axis_index("prow")
    q = lax.axis_index("pcol")
    x = q // 8
    z = q % 8
    par = p % 2
    sib = p + 1 - 2 * par

    def zat(d):
        return 8 * x + lax.rem(z + d + 16, 8)

    def xat(d):
        return lax.rem(q + 8 * d + 64, 32)

    barrier = pltpu.get_barrier_semaphore()

    def greet(pp, qq):
        pl.semaphore_signal(barrier, inc=1, device_id=(pp, qq), device_id_type=MESH)

    y = p // 2
    for d in range(1, 8):
        greet(lax.rem(p + d, 8), q)
        greet(p, zat(d))
    for d in (1, 2, 3):
        greet(p, xat(d))
    count = jnp.int32(17)

    from_p, from_q = lax.rem(z - p + 8, 4), 8 * x + p
    from_self = (p == 0) & (z == 0)

    def scatter_to(c):
        return z, 8 * x + lax.rem(z + 4 * c + p, 8)

    def scatter_self(c):
        return (p == 0) & (z == 0) & (c == 0)

    def greet_if(cond, pp, qq):
        pl.when(cond)(functools.partial(greet, pp, qq))
        return jnp.where(cond, 1, 0)

    count = count + greet_if(jnp.logical_not(from_self), from_p, from_q)
    for c in range(2):
        count = count + greet_if((p < NP) & jnp.logical_not(scatter_self(c)), *scatter_to(c))

    tiles = ((0, 0, 0), (0, 1, 0), (0, 2, 1), (0, 3, 2), (1, 1, 3),
             (1, 2, 0), (1, 3, 1), (2, 2, 2), (2, 3, 3), (3, 3, 0))
    origin_dev = (p < NP) & (p <= q) & (q < NP)
    plane = jnp.int32(0)
    my_tile = jnp.int32(0)
    for t, (k, kc, yt) in enumerate(tiles):
        me = (p == k) & (q == kc)
        plane = jnp.where(me, yt, plane)
        my_tile = jnp.where(me, t, my_tile)
        count = count + greet_if((x == 0) & (y == yt) & jnp.logical_not(me), k, kc)

    def piece_targets():
        for c in range(2):
            for d in range(8):
                yield c, d, (2 * plane + c), lax.rem(z + d, 8)

    for c, d, pp, qq in piece_targets():
        cond = origin_dev & jnp.logical_not((p == pp) & (q == qq))
        count = count + greet_if(cond, pp, qq)
    relay0 = (x == 0) & (y == 0)
    count = count + greet_if(jnp.logical_not(relay0), par, z)

    def relay_targets():
        for dy in range(4):
            for dx in range(4):
                if dx or dy:
                    yield 4 * dy + dx, 2 * lax.rem(y + dy, 4) + par, xat(dx)

    for _, pp, qq in relay_targets():
        count = count + greet_if(relay0, pp, qq)
    pl.semaphore_wait(barrier, count)

    def send(src, dst, ssem, rsem, pp, qq):
        return pltpu.make_async_remote_copy(
            src_ref=src, dst_ref=dst, send_sem=ssem, recv_sem=rsem,
            device_id=(pp, qq), device_id_type=MESH,
        )

    def tile(i):
        return pl.ds(pl.multiple_of(i * B, B), B)

    def gslot(k, c):
        return g_ref.at[tile(k), pl.ds(c * B, B)]

    def origin(c):
        for n, d in enumerate((2, 6, None)):
            pp = sib if d is None else lax.rem(p + d, 8)
            yield send(a_ref.at[c], gslot(p, c), so.at[c, n], rg.at[p, c], pp, q)

    def relay(k, c):
        return send(gslot(k, c), gslot(k, c), sf.at[k, c], rg.at[k, c], sib, q)

    def onward(i, c):
        k = par + 2 * i
        pp = lax.rem(p + (2 if c == 0 else 6), 8)
        return y == (i + (1 if c == 0 else 3)) % 4, send(
            gslot(k, c), gslot(k, c), sg.at[i, c], rg.at[k, c], pp, q)

    def relay_event(i, c, far):
        k = par + 2 * i
        opposite = y == (i + 2) % 4

        @pl.when(opposite if far else (k != p) & jnp.logical_not(opposite))
        def _():
            relay(k, c).wait_recv()
            relay(k, c).start()
            if not far:
                cond, cp = onward(i, c)
                pl.when(cond)(cp.start)

    def mpart(t, lo, n):
        k, kc, _ = tiles[t]
        return m_ref.at[pl.ds(pl.multiple_of(k * B + lo, 16), n), pl.ds(kc * B, B)]

    def one_piece(c, d, pp, qq):
        lo = pl.multiple_of(c * 128 + 16 * qq, 16)
        dst = m_ref.at[pl.ds(pl.multiple_of(p * B + c * 128 + 16 * qq, 16), 16), tile(q)]
        return send(a_ref.at[0, pl.ds(lo, 16), :], dst, s1.at[c, d], r1.at[my_tile], pp, qq)

    def each_piece(act):
        for c, d, pp, qq in piece_targets():
            cp = one_piece(c, d, pp, qq)
            if d == 0:
                pl.when((p != pp))(functools.partial(act, cp))
            else:
                act(cp)

    my_lo = par * 128 + 16 * z

    def my_piece(t):
        return mpart(t, my_lo, 16)

    def got_piece(t, ref, rsem):
        send(ref, ref, s1.at[0, 0], rsem, sib, q).wait_recv()

    def relay_sends(t):
        if t == 0:
            for n, pp, qq in relay_targets():
                yield send(my_piece(t), my_piece(t), s2.at[n], r2.at[t], pp, qq)
        else:
            for n in range(3):
                yield send(my_piece(t), my_piece(t), s2b.at[t, n], r2.at[t], p, xat(n + 1))

    def relay_tile(t):
        k, kc, yt = tiles[t]

        @pl.when((x == 0) & (y == yt))
        def _():
            @pl.when(jnp.logical_not((p == k) & (q == kc)))
            def _():
                got_piece(t, my_piece(t), r1.at[t])
            for cp in relay_sends(t):
                cp.start()

    def in_plane(t):
        return None if t == 0 else y == tiles[t][2]

    def when(cond, f):
        if cond is None:
            f()
        else:
            pl.when(cond)(f)

    def ring_send(t, d):
        return send(my_piece(t), my_piece(t), s3.at[t, d], r3.at[t, z], p, zat(d))

    def ring_tile(t):
        def go():
            @pl.when(jnp.logical_not((x == 0) & (y == tiles[t][2])))
            def _():
                got_piece(t, my_piece(t), r2.at[t])
            for d in (4, 3, 5, 2, 6, 1, 7):
                ring_send(t, d).start()
        when(in_plane(t), go)

    def half_send(t, c):
        part = mpart(t, c * 128, 128)
        return send(part, part, s4.at[t], r4.at[t], sib, q)

    def plane_sends(t):
        part = mpart(t, par * 128, 128)
        for n in range(3):
            yield send(part, part, s5.at[t, n], r5.at[t], lax.rem(p + 2 * n + 2, 8), q)

    def half_tile(t):
        def go():
            for d in range(1, 8):
                w = lax.rem(z + d, 8)
                got_piece(t, mpart(t, par * 128 + 16 * w, 16), r3.at[t, w])
            if t:
                for cp in plane_sends(t):
                    cp.start()
            half_send(t, par).start()
        when(in_plane(t), go)

    def pass_tile(t):
        @pl.when(y != tiles[t][2])
        def _():
            got_piece(t, mpart(t, par * 128, 128), r5.at[t])
            half_send(t, par).start()

    def half_got(t):
        half_send(t, 1 - par).wait_recv()

    s = 1 - 2 * par

    def xm(d):
        return lax.rem(x + d + 4, 4)

    def zm(d):
        return lax.rem(z + d + 16, 8)

    def scatter(c, b):
        pp, qq = scatter_to(c)
        rows = pl.ds(HA, HB) if b else pl.ds(0, HA)
        return send(at.at[c, rows, :], bulk.at[lax.rem(z + 4 * c + p, 8), x, rows, :],
                    ss.at[c, b], rt.at[b], pp, qq)

    def hop(ref, ssem, rsem, to):
        return send(ref, ref, ssem, rsem, p, to)

    def got(ref, rsem):
        hop(ref, saz.at[0], rsem, xat(1)).wait_recv()

    def part_a(zz, xx):
        return bulk.at[zz, xx, pl.ds(0, HA), :]

    def half_a(zz, xx, h):
        return bulk.at[zz, xx, pl.ds(h * (HA // 2), HA // 2), :]

    def part_b(zz, xx):
        return bulk.at[zz, xx, pl.ds(HA, HB), :]

    def row_b(zz):
        return bulk.at[zz, :, pl.ds(HA, HB), :]

    def az(n, way):
        w = s * way
        zz = zm(-n * w)
        return hop(part_a(zz, x), saz.at[n if way > 0 else 4 + n], ra.at[zz, x], zat(w))

    def bz(n, way):
        w = s * way
        zz = zm(-n * w)
        return hop(row_b(zz), sbz.at[n if way > 0 else 4 + n], rb.at[zz], zat(w))

    def ax(dz, way):
        zz = zm(dz)
        return hop(part_a(zz, x), sax.at[dz % 8, 0 if way > 0 else 1], ra.at[zz, x], xat(way))

    def axf(dz, way):
        zz = zm(dz)
        h = 0 if way > 0 else 1
        return hop(half_a(zz, xm(-way), h), sax.at[dz % 8, 2 + h], rah.at[zz, h], xat(way))

    def bx(n):
        return hop(part_b(z, x), sbx.at[n], rbx.at[x], xat(n + 1))

    def last(way):
        return 4 if way > 0 else 3

    def arrive(b):
        rows = pl.ds(HA, HB) if b else pl.ds(0, HA)
        own = bulk.at[z, x, rows, :]

        @pl.when(from_self)
        def _():
            cp = pltpu.make_async_copy(at.at[0, rows, :], own, rt.at[b])
            cp.start()
            cp.wait()

        @pl.when(jnp.logical_not(from_self))
        def _():
            send(own, own, ss.at[0, b], rt.at[b], from_p, from_q).wait_recv()

    def start_b_event():
        arrive(1)
        for n in (0, 2, 1):
            bx(n).start()

    def start_event():
        arrive(0)
        for way in (1, -1):
            az(0, way).start()
        for way in (1, -1):
            ax(0, way).start()

    def az_event(n):
        for way in (1, -1):
            if n <= last(way):
                zz = zm(-n * s * way)
                got(part_a(zz, x), ra.at[zz, x])
                if n < last(way):
                    az(n, way).start()
        for dz in ((n, -n) if n < 4 else (4,)):
            for way in (1, -1):
                ax(dz, way).start()

    def bx_event():
        for dx in (1, -1, 2):
            got(part_b(z, xm(dx)), rbx.at[xm(dx)])
        for way in (1, -1):
            bz(0, way).start()

    def bz_event(n):
        for way in (1, -1):
            if n <= last(way):
                zz = zm(-n * s * way)
                got(row_b(zz), rb.at[zz])
                if n < last(way):
                    bz(n, way).start()

    def ax_event(dz):
        zz = zm(dz)
        for way in (1, -1):
            got(part_a(zz, xm(-way)), ra.at[zz, xm(-way)])
            axf(dz, way).start()

    def ax2_event(dz):
        zz = zm(dz)
        for h in range(2):
            got(half_a(zz, xm(2), h), rah.at[zz, h])

    E = functools.partial
    def strips_event():
        @pl.when(p < NP)
        def _():
            for c in range(2):
                for cp in origin(c):
                    cp.start()
                g_ref[tile(p), c * B:(c + 1) * B] = a_ref[c]

    events = {
        (0, 0): [E(half_tile, t) for t in (1, 2, 3, 4)],
        (0, 2): [E(half_tile, t) for t in (5, 6, 7, 8, 9)],
        (0, 5): [E(pass_tile, t) for t in (1, 2, 3, 4)],
        (0, 6): [strips_event],
        (0, 7): [E(az_event, 1)],
        (1, 0): [E(pass_tile, t) for t in (5, 6, 7, 8, 9)] + [E(bz_event, 1)],
        (1, 4): [E(ax_event, 0)],
        (1, 5): [E(az_event, 2)],
        (1, 7): [E(relay_event, i, c, False) for c in range(2) for i in range(2)],
        (2, 0): [E(bz_event, 2), E(ax_event, 1), E(ax_event, -1)],
        (2, 3): [E(az_event, 3)],
        (2, 5): [E(relay_event, i, c, True) for c in range(2) for i in range(2)],
        (2, 6): [E(ax_event, 2), E(ax_event, -2)],
        (3, 0): [E(bz_event, 3)],
        (3, 1): [E(az_event, 4)],
        (3, 3): [E(ax_event, 3), E(ax_event, -3)],
        (3, 7): [E(ax_event, 4)],
    }

    def scatter_start():
        at[0] = a_ref[0].T
        at[1] = a_ref[1].T
        for b in (1, 0):
            for c in range(2):
                pl.when(jnp.logical_not(scatter_self(c)))(scatter(c, b).start)

    @pl.when(origin_dev)
    def _():
        each_piece(lambda cp: cp.start())

        @pl.when(plane == y)
        def _():
            lo = pl.multiple_of(my_lo, 16)
            m_ref[pl.ds(pl.multiple_of(p * B + my_lo, 16), 16), tile(q)] = a_ref[0, pl.ds(lo, 16), :]
    pl.when(p < NP)(scatter_start)
    relay_tile(0)
    ring_tile(0)
    for t in range(1, 10):
        relay_tile(t)
    S[...] = jnp.zeros_like(S)
    start_b_event()
    half_tile(0)
    for t in range(1, 10):
        ring_tile(t)
    start_event()
    bx_event()

    row = lax.broadcasted_iota(jnp.int32, (B, B), 0)
    col = lax.broadcasted_iota(jnp.int32, (B, B), 1)

    def step(k, _):
        for t, (kk, kc, _) in enumerate(tiles):
            if kk == kc:
                pl.when(k == kk)(functools.partial(half_got, t))

        T[...] = S[tile(k), tile(k)] + m_ref[tile(k), tile(k)]

        def between(jb):
            for kk in range(NP):
                for ev in events.get((kk, jb), ()):
                    pl.when(k == kk)(ev)

        factor_tile(T, between)
        S[tile(k), tile(k)] = T[...]
        X = jnp.where(row >= col, T[...], 0.0)
        for t, (kk, kc, _) in enumerate(tiles):
            if kk != kc:
                pl.when(k == kk)(functools.partial(half_got, t))

        def solve(m, _):
            S[tile(k), tile(m)] = dot3(X, S[tile(k), tile(m)] + m_ref[tile(k), tile(m)])
            return 0

        lax.fori_loop(k + 1, NP, solve, 0)

        def trail(i, _):
            left = S[tile(k), tile(i)].T

            def inner(m, _):
                S[tile(i), tile(m)] = S[tile(i), tile(m)] - dot3(left, S[tile(k), tile(m)])
                return 0

            lax.fori_loop(i, NP, inner, 0)
            return 0

        lax.fori_loop(k + 1, NP, trail, 0)
        return 0

    lax.fori_loop(0, NP, step, 0)

    for i in range(2):
        for c in range(2):
            relay(1 - par + 2 * i, c).wait_recv()

    def block(i, j):
        return S[i * B:(i + 1) * B, j * B:(j + 1) * B]

    for k in range(NP):
        acc = g_ref[k * B:(k + 1) * B, :]
        for i in range(k):
            acc = acc - dot3(block(i, k).T, W[i * B:(i + 1) * B, :])
        W[k * B:(k + 1) * B, :] = dot3(jnp.where(row >= col, block(k, k), 0.0), acc)

    kq = jnp.minimum(q, NP - 1)
    kp = jnp.minimum(p, NP - 1)
    u = S[tile(kq), tile(kp)]
    u_diag = jnp.where(col > row, u, jnp.where(col == row, 1.0 / u, 0.0))
    u = jnp.where(kp == kq, u_diag, jnp.where(kq < kp, u, 0.0))
    l_ref[...] = u.T

    col2 = lax.broadcasted_iota(jnp.int32, (B, 2 * B), 1)
    row2 = lax.broadcasted_iota(jnp.int32, (B, 2 * B), 0)
    for k in (3, 2, 1, 0):
        unit = jnp.where((row2 == col2) & (q == k), 1.0, 0.0)
        acc = jnp.where((col2 < B) & (q < NP), unit, W[k * B:(k + 1) * B, :])
        for m in range(k + 1, NP):
            acc = acc - dot3(S[k * B:(k + 1) * B, m * B:(m + 1) * B], W[m * B:(m + 1) * B, :])
        X = jnp.where(row >= col, S[k * B:(k + 1) * B, k * B:(k + 1) * B], 0.0)
        w = dot3(X.T, acc)
        W[k * B:(k + 1) * B, :] = w
        hi, lo = split(w)
        whi_ref[k * B:(k + 1) * B, :] = hi
        wlo_ref[k * B:(k + 1) * B, :] = lo

    bz_event(4)
    for dz in range(8):
        ax2_event(dz)

    @pl.when(p < NP)
    def _():
        for c in range(2):
            for cp in origin(c):
                cp.wait_send()
            for b in (1, 0):
                pl.when(jnp.logical_not(scatter_self(c)))(scatter(c, b).wait_send)
    for c in range(2):
        for i in range(2):
            k = par + 2 * i
            pl.when(k != p)(relay(k, c).wait_send)
            cond, cp = onward(i, c)
            pl.when(cond)(cp.wait_send)
    pl.when(origin_dev)(lambda: each_piece(lambda cp: cp.wait_send()))
    for t in range(10):
        @pl.when((x == 0) & (y == tiles[t][2]))
        def _():
            for cp in relay_sends(t):
                cp.wait_send()

        def drain():
            for d in range(1, 8):
                ring_send(t, d).wait_send()
            if t:
                for cp in plane_sends(t):
                    cp.wait_send()
        when(in_plane(t), drain)
        half_send(t, par).wait_send()
    for n in range(3):
        bx(n).wait_send()
    for way in (1, -1):
        for n in range(last(way)):
            az(n, way).wait_send()
            bz(n, way).wait_send()
        for dz in range(8):
            ax(dz, way).wait_send()
            axf(dz, way).wait_send()


def main(a):
    dma = pltpu.SemaphoreType.DMA
    vmem = pl.BlockSpec(memory_space=pltpu.VMEM)
    return pl.pallas_call(
        main_kernel,
        out_shape=(
            jax.ShapeDtypeStruct((8, 4, B, B), F32),
            jax.ShapeDtypeStruct((TOP, 2 * B), BF16),
            jax.ShapeDtypeStruct((TOP, 2 * B), BF16),
            jax.ShapeDtypeStruct((B, B), F32),
        ),
        in_specs=[vmem],
        out_specs=[vmem] * 4,
        scratch_shapes=[
            pltpu.VMEM((2, B, B), F32),
            pltpu.VMEM((TOP, TOP), F32),
            pltpu.VMEM((TOP, 2 * B), F32),
            pltpu.VMEM((TOP, TOP), F32),
            pltpu.VMEM((B, B), F32),
            pltpu.VMEM((TOP, 2 * B), F32),
            dma((NP, 2)), dma((2, 3)), dma((NP, 2)), dma((2, 2)),
            dma((10,)), dma((10,)), dma((10, 8)), dma((10,)), dma((10,)),
            dma((2, 8)), dma((16,)), dma((10, 3)), dma((10, 8)), dma((10,)), dma((10, 3)),
            dma((2,)), dma((2, 2)), dma((8, 4)), dma((8, 2)), dma((8,)), dma((4,)),
            dma((7,)), dma((8, 4)), dma((3,)), dma((7,)),
        ],
        compiler_params=pltpu.CompilerParams(
            collective_id=1, has_side_effects=True, vmem_limit_bytes=30 * 1024 * 1024),
        cost_estimate=pl.CostEstimate(
            flops=60_000_000_000, bytes_accessed=8_000_000, transcendentals=0),
        name="main",
    )(a)


RG = 2


def update_kernel(p_ref, b_ref, m_ref, whi_ref, wlo_ref, l_ref, o_ref):
    first = pl.program_id(0) * RG
    p = p_ref[0]
    q = p_ref[1]

    def row_tile(r):
        return jnp.concatenate(
            [b_ref[(p + 4 * (r // 4) + k) % 8, r % 4].astype(BF16) for k in range(NP)], axis=1)

    left = jnp.concatenate([row_tile(first + n) for n in range(RG)], axis=0)
    acc = dot1(left, whi_ref[...]) + dot1(left, wlo_ref[...])
    factor_col = q < NP
    for n in range(RG):
        top = (first + n == 0) & (p < NP)
        m = m_ref[pl.ds(pl.multiple_of((first + n) * B, B), B)].astype(F32)
        a0 = acc[n * B:(n + 1) * B, 0:B]
        a1 = acc[n * B:(n + 1) * B, B:]
        c0 = jnp.where(factor_col, a0, m[:, 0, :] - a0)
        c0 = jnp.where(top, jnp.where(factor_col, l_ref[...], 0.0), c0)
        c1 = jnp.where(top, 0.0, m[:, 1, :] - a1)
        for h, part in enumerate((c0[:, :128], c0[:, 128:], c1[:, :128], c1[:, 128:])):
            o_ref[pl.ds(4 * B * n + h, B, stride=4), :] = part


def update(place, bulk, mine, whi, wlo, ltile):
    vmem = pl.BlockSpec(memory_space=pltpu.VMEM)
    return pl.pallas_call(
        update_kernel,
        out_shape=jax.ShapeDtypeStruct((8 * 4 * B, 128), F32),
        grid_spec=pltpu.PrefetchScalarGridSpec(
            num_scalar_prefetch=1,
            grid=(8 // RG,),
            in_specs=[vmem] * 5,
            out_specs=pl.BlockSpec((4 * B * RG, 128), lambda r, place: (r, 0)),
        ),
        compiler_params=pltpu.CompilerParams(vmem_limit_bytes=24 * 1024 * 1024),
        cost_estimate=pl.CostEstimate(
            flops=4_300_000_000, bytes_accessed=16_000_000, transcendentals=0),
        name="update",
    )(place, bulk, mine, whi, wlo, ltile)


def local(covariance):
    mine = covariance.reshape(8, B, 2, B)
    a = mine[0].astype(F32).transpose(1, 0, 2)
    mine = mine.reshape(8 * B, 2, B)
    bulk, whi, wlo, ltile = main(a)
    place = jnp.stack([lax.axis_index("prow"), lax.axis_index("pcol")]).astype(jnp.int32)
    out = update(place, bulk, mine, whi, wlo, ltile)
    return out.reshape(8, 1, B, 2, 1, B)


def solution(mesh):
    in_specs = (P(None, "prow", None, None, "pcol", None),)
    out_specs = P(None, "prow", None, None, "pcol", None)
    return jax.shard_map(local, mesh=mesh, in_specs=in_specs, out_specs=out_specs, check_vma=False)
```

```python
import functools
import jax
import jax.numpy as jnp
from jax import lax
from jax.experimental import pallas as pl
from jax.experimental.pallas import tpu as pltpu
from jax.sharding import PartitionSpec as P

B = 256
NP = 4
TOP = NP * B
F32 = jnp.float32
BF16 = jnp.bfloat16
MESH = pl.DeviceIdType.MESH


def split(a):
    hi = a.astype(BF16)
    return hi, (a - hi.astype(F32)).astype(BF16)


def dot1(a, b):
    return jnp.dot(a, b, preferred_element_type=F32)


def dot3(a, b):
    ah, al = split(a)
    bh, bl = split(b)
    return dot1(ah, bh) + (dot1(ah, bl) + dot1(al, bh))


def panel(R, j, sub, lane):
    for g in range(4):
        c0 = j + 8 * g
        lt = c0 // 128
        o = c0 % 128
        cb = {}
        for h in range(g, 4):
            for t in range(8):
                cb[h, t] = jnp.broadcast_to(R[h][lt][:, o + t:o + t + 1], (8, 128))
        inblk = (lane >= o) & (lane < o + 8)
        R[g][lt] = jnp.where(inblk, jnp.where(lane - o == sub, 1.0, 0.0), R[g][lt])
        for h in range(g + 1, 4):
            R[h][lt] = jnp.where(inblk, 0.0, R[h][lt])
        scale = jnp.zeros((8, 128), F32)
        for t in range(8):
            piv = jnp.broadcast_to(cb[g, t][t:t + 1, :], (8, 128))
            inv = 1.0 / piv
            scale = jnp.where(sub == t, lax.rsqrt(piv), scale)
            rows = [jnp.broadcast_to(R[g][l][t:t + 1, :], (8, 128)) for l in range(2)]
            crow = {u: jnp.broadcast_to(cb[g, u][t:t + 1, :], (8, 128)) for u in range(t + 1, 8)}
            for h in range(g, 4):
                f = cb[h, t] * inv
                if h == g:
                    f = jnp.where(sub > t, f, 0.0)
                for l in range(2):
                    R[h][l] = R[h][l] - f * rows[l]
                for u in range(t + 1, 8):
                    cb[h, u] = cb[h, u] - f * crow[u]
        for u in range(1, 8):
            R[g][lt] = jnp.where((lane == o + u) & (sub < u), cb[g, u], R[g][lt])
        for l in range(2):
            R[g][l] = R[g][l] * scale
    return R


def factor_tile(T, between):
    sub = lax.broadcasted_iota(jnp.int32, (8, 128), 0)
    lane = lax.broadcasted_iota(jnp.int32, (8, 128), 1)
    pr = lax.broadcasted_iota(jnp.int32, (32, B), 0)
    pc = lax.broadcasted_iota(jnp.int32, (32, B), 1)
    for jb in range(8):
        between(jb)
        j = 32 * jb
        R = [[T[j + 8 * g:j + 8 * g + 8, 128 * l:128 * l + 128] for l in range(2)] for g in range(4)]
        R = panel(R, j, sub, lane)
        rows = jnp.concatenate([jnp.concatenate(r, axis=1) for r in R], axis=0)
        T[j:j + 32, :] = rows
        if jb < 7:
            left = rows.T[j + 32:, :]
            n = B - j - 32
            ln = lax.broadcasted_iota(jnp.int32, (n, B), 1)
            low = jnp.where((ln >= j) & (ln < j + 32), 0.0, T[j + 32:, :])
            rows = jnp.where((pc < j + 32) & (pc > j + pr), 0.0, rows)
            T[j + 32:, :] = low - dot3(left, rows)


HA = 160
HB = B - HA


def main_kernel(a_ref, bulk, whi_ref, wlo_ref, l_ref,
                at, m_ref, g_ref, S, T, W,
                rg, so, sf, sg, r1, r2, r3, r4, r5, s1, s2, s2b, s3, s4, s5,
                rt, ss, ra, rah, rb, rbx, saz, sax, sbx, sbz):
    p = lax.axis_index("prow")
    q = lax.axis_index("pcol")
    x = q // 8
    z = q % 8
    par = p % 2
    sib = p + 1 - 2 * par

    def zat(d):
        return 8 * x + lax.rem(z + d + 16, 8)

    def xat(d):
        return lax.rem(q + 8 * d + 64, 32)

    barrier = pltpu.get_barrier_semaphore()

    def greet(pp, qq):
        pl.semaphore_signal(barrier, inc=1, device_id=(pp, qq), device_id_type=MESH)

    y = p // 2
    for d in range(1, 8):
        greet(lax.rem(p + d, 8), q)
        greet(p, zat(d))
    for d in (1, 2, 3):
        greet(p, xat(d))
    count = jnp.int32(17)

    from_p, from_q = lax.rem(z - p + 8, 4), 8 * x + p
    from_self = (p == 0) & (z == 0)

    def scatter_to(c):
        return z, 8 * x + lax.rem(z + 4 * c + p, 8)

    def scatter_self(c):
        return (p == 0) & (z == 0) & (c == 0)

    def greet_if(cond, pp, qq):
        pl.when(cond)(functools.partial(greet, pp, qq))
        return jnp.where(cond, 1, 0)

    count = count + greet_if(jnp.logical_not(from_self), from_p, from_q)
    for c in range(2):
        count = count + greet_if((p < NP) & jnp.logical_not(scatter_self(c)), *scatter_to(c))

    tiles = ((0, 0, 0), (0, 1, 0), (0, 2, 1), (0, 3, 2), (1, 1, 3),
             (1, 2, 0), (1, 3, 1), (2, 2, 2), (2, 3, 3), (3, 3, 0))
    origin_dev = (p < NP) & (p <= q) & (q < NP)
    plane = jnp.int32(0)
    my_tile = jnp.int32(0)
    for t, (k, kc, yt) in enumerate(tiles):
        me = (p == k) & (q == kc)
        plane = jnp.where(me, yt, plane)
        my_tile = jnp.where(me, t, my_tile)
        count = count + greet_if((x == 0) & (y == yt) & jnp.logical_not(me), k, kc)

    def piece_targets():
        for c in range(2):
            for d in range(8):
                yield c, d, (2 * plane + c), lax.rem(z + d, 8)

    for c, d, pp, qq in piece_targets():
        cond = origin_dev & jnp.logical_not((p == pp) & (q == qq))
        count = count + greet_if(cond, pp, qq)
    relay0 = (x == 0) & (y == 0)
    count = count + greet_if(jnp.logical_not(relay0), par, z)

    def relay_targets():
        for dy in range(4):
            for dx in range(4):
                if dx or dy:
                    yield 4 * dy + dx, 2 * lax.rem(y + dy, 4) + par, xat(dx)

    for _, pp, qq in relay_targets():
        count = count + greet_if(relay0, pp, qq)
    pl.semaphore_wait(barrier, count)

    def send(src, dst, ssem, rsem, pp, qq):
        return pltpu.make_async_remote_copy(
            src_ref=src, dst_ref=dst, send_sem=ssem, recv_sem=rsem,
            device_id=(pp, qq), device_id_type=MESH,
        )

    def tile(i):
        return pl.ds(pl.multiple_of(i * B, B), B)

    def gslot(k, c):
        return g_ref.at[tile(k), pl.ds(c * B, B)]

    def origin(c):
        for n, d in enumerate((2, 6, None)):
            pp = sib if d is None else lax.rem(p + d, 8)
            yield send(a_ref.at[c], gslot(p, c), so.at[c, n], rg.at[p, c], pp, q)

    def relay(k, c):
        return send(gslot(k, c), gslot(k, c), sf.at[k, c], rg.at[k, c], sib, q)

    def onward(i, c):
        k = par + 2 * i
        pp = lax.rem(p + (2 if c == 0 else 6), 8)
        return y == (i + (1 if c == 0 else 3)) % 4, send(
            gslot(k, c), gslot(k, c), sg.at[i, c], rg.at[k, c], pp, q)

    def relay_event(i, c, far):
        k = par + 2 * i
        opposite = y == (i + 2) % 4

        @pl.when(opposite if far else (k != p) & jnp.logical_not(opposite))
        def _():
            relay(k, c).wait_recv()
            relay(k, c).start()
            if not far:
                cond, cp = onward(i, c)
                pl.when(cond)(cp.start)

    def mpart(t, lo, n):
        k, kc, _ = tiles[t]
        return m_ref.at[pl.ds(pl.multiple_of(k * B + lo, 16), n), pl.ds(kc * B, B)]

    def one_piece(c, d, pp, qq):
        lo = pl.multiple_of(c * 128 + 16 * qq, 16)
        dst = m_ref.at[pl.ds(pl.multiple_of(p * B + c * 128 + 16 * qq, 16), 16), tile(q)]
        return send(a_ref.at[0, pl.ds(lo, 16), :], dst, s1.at[c, d], r1.at[my_tile], pp, qq)

    def each_piece(act):
        for c, d, pp, qq in piece_targets():
            cp = one_piece(c, d, pp, qq)
            if d == 0:
                pl.when((p != pp))(functools.partial(act, cp))
            else:
                act(cp)

    my_lo = par * 128 + 16 * z

    def my_piece(t):
        return mpart(t, my_lo, 16)

    def got_piece(t, ref, rsem):
        send(ref, ref, s1.at[0, 0], rsem, sib, q).wait_recv()

    def relay_sends(t):
        if t == 0:
            for n, pp, qq in relay_targets():
                yield send(my_piece(t), my_piece(t), s2.at[n], r2.at[t], pp, qq)
        else:
            for n in range(3):
                yield send(my_piece(t), my_piece(t), s2b.at[t, n], r2.at[t], p, xat(n + 1))

    def relay_tile(t):
        k, kc, yt = tiles[t]

        @pl.when((x == 0) & (y == yt))
        def _():
            @pl.when(jnp.logical_not((p == k) & (q == kc)))
            def _():
                got_piece(t, my_piece(t), r1.at[t])
            for cp in relay_sends(t):
                cp.start()

    def in_plane(t):
        return None if t == 0 else y == tiles[t][2]

    def when(cond, f):
        if cond is None:
            f()
        else:
            pl.when(cond)(f)

    def ring_send(t, d):
        return send(my_piece(t), my_piece(t), s3.at[t, d], r3.at[t, z], p, zat(d))

    def ring_tile(t):
        def go():
            @pl.when(jnp.logical_not((x == 0) & (y == tiles[t][2])))
            def _():
                got_piece(t, my_piece(t), r2.at[t])
            for d in (4, 3, 5, 2, 6, 1, 7):
                ring_send(t, d).start()
        when(in_plane(t), go)

    def half_send(t, c):
        part = mpart(t, c * 128, 128)
        return send(part, part, s4.at[t], r4.at[t], sib, q)

    def plane_sends(t):
        part = mpart(t, par * 128, 128)
        for n in range(3):
            yield send(part, part, s5.at[t, n], r5.at[t], lax.rem(p + 2 * n + 2, 8), q)

    def half_tile(t):
        def go():
            for d in range(1, 8):
                w = lax.rem(z + d, 8)
                got_piece(t, mpart(t, par * 128 + 16 * w, 16), r3.at[t, w])
            if t:
                for cp in plane_sends(t):
                    cp.start()
            half_send(t, par).start()
        when(in_plane(t), go)

    def pass_tile(t):
        @pl.when(y != tiles[t][2])
        def _():
            got_piece(t, mpart(t, par * 128, 128), r5.at[t])
            half_send(t, par).start()

    def half_got(t):
        half_send(t, 1 - par).wait_recv()

    s = 1 - 2 * par

    def xm(d):
        return lax.rem(x + d + 4, 4)

    def zm(d):
        return lax.rem(z + d + 16, 8)

    def scatter(c, b):
        pp, qq = scatter_to(c)
        rows = pl.ds(HA, HB) if b else pl.ds(0, HA)
        return send(at.at[c, rows, :], bulk.at[lax.rem(z + 4 * c + p, 8), x, rows, :],
                    ss.at[c, b], rt.at[b], pp, qq)

    def hop(ref, ssem, rsem, to):
        return send(ref, ref, ssem, rsem, p, to)

    def got(ref, rsem):
        hop(ref, saz.at[0], rsem, xat(1)).wait_recv()

    def part_a(zz, xx):
        return bulk.at[zz, xx, pl.ds(0, HA), :]

    def half_a(zz, xx, h):
        return bulk.at[zz, xx, pl.ds(h * (HA // 2), HA // 2), :]

    def part_b(zz, xx):
        return bulk.at[zz, xx, pl.ds(HA, HB), :]

    def row_b(zz):
        return bulk.at[zz, :, pl.ds(HA, HB), :]

    def az(n, way):
        w = s * way
        zz = zm(-n * w)
        return hop(part_a(zz, x), saz.at[n if way > 0 else 4 + n], ra.at[zz, x], zat(w))

    def bz(n, way):
        w = s * way
        zz = zm(-n * w)
        return hop(row_b(zz), sbz.at[n if way > 0 else 4 + n], rb.at[zz], zat(w))

    def ax(dz, way):
        zz = zm(dz)
        return hop(part_a(zz, x), sax.at[dz % 8, 0 if way > 0 else 1], ra.at[zz, x], xat(way))

    def axf(dz, way):
        zz = zm(dz)
        h = 0 if way > 0 else 1
        return hop(half_a(zz, xm(-way), h), sax.at[dz % 8, 2 + h], rah.at[zz, h], xat(way))

    def bx(n):
        return hop(part_b(z, x), sbx.at[n], rbx.at[x], xat(n + 1))

    def last(way):
        return 4 if way > 0 else 3

    def arrive(b):
        rows = pl.ds(HA, HB) if b else pl.ds(0, HA)
        own = bulk.at[z, x, rows, :]

        @pl.when(from_self)
        def _():
            cp = pltpu.make_async_copy(at.at[0, rows, :], own, rt.at[b])
            cp.start()
            cp.wait()

        @pl.when(jnp.logical_not(from_self))
        def _():
            send(own, own, ss.at[0, b], rt.at[b], from_p, from_q).wait_recv()

    def start_b_event():
        arrive(1)
        for n in (0, 2, 1):
            bx(n).start()

    def start_event():
        arrive(0)
        for way in (1, -1):
            az(0, way).start()
        for way in (1, -1):
            ax(0, way).start()

    def az_event(n):
        for way in (1, -1):
            if n <= last(way):
                zz = zm(-n * s * way)
                got(part_a(zz, x), ra.at[zz, x])
                if n < last(way):
                    az(n, way).start()
        for dz in ((n, -n) if n < 4 else (4,)):
            for way in (1, -1):
                ax(dz, way).start()

    def bx_event():
        for dx in (1, -1, 2):
            got(part_b(z, xm(dx)), rbx.at[xm(dx)])
        for way in (1, -1):
            bz(0, way).start()

    def bz_event(n):
        for way in (1, -1):
            if n <= last(way):
                zz = zm(-n * s * way)
                got(row_b(zz), rb.at[zz])
                if n < last(way):
                    bz(n, way).start()

    def ax_event(dz):
        zz = zm(dz)
        for way in (1, -1):
            got(part_a(zz, xm(-way)), ra.at[zz, xm(-way)])
            axf(dz, way).start()

    def ax2_event(dz):
        zz = zm(dz)
        for h in range(2):
            got(half_a(zz, xm(2), h), rah.at[zz, h])

    E = functools.partial
    def strips_event():
        @pl.when(p < NP)
        def _():
            for c in range(2):
                for cp in origin(c):
                    cp.start()
                g_ref[tile(p), c * B:(c + 1) * B] = a_ref[c]

    events = {
        (0, 0): [E(half_tile, t) for t in (1, 2, 3, 4)],
        (0, 2): [E(half_tile, t) for t in (5, 6, 7, 8, 9)],
        (0, 5): [E(pass_tile, t) for t in (1, 2, 3, 4)],
        (0, 6): [strips_event],
        (0, 7): [E(az_event, 1)],
        (1, 0): [E(pass_tile, t) for t in (5, 6, 7, 8, 9)] + [E(bz_event, 1)],
        (1, 4): [E(ax_event, 0)],
        (1, 5): [E(az_event, 2)],
        (1, 7): [E(relay_event, i, c, False) for c in range(2) for i in range(2)],
        (2, 0): [E(bz_event, 2), E(ax_event, 1), E(ax_event, -1)],
        (2, 3): [E(az_event, 3)],
        (2, 5): [E(relay_event, i, c, True) for c in range(2) for i in range(2)],
        (2, 6): [E(ax_event, 2), E(ax_event, -2)],
        (3, 0): [E(bz_event, 3)],
        (3, 1): [E(az_event, 4)],
        (3, 3): [E(ax_event, 3), E(ax_event, -3)],
        (3, 7): [E(ax_event, 4)],
    }

    def scatter_start():
        at[0] = a_ref[0].T
        at[1] = a_ref[1].T
        for b in (1, 0):
            for c in range(2):
                pl.when(jnp.logical_not(scatter_self(c)))(scatter(c, b).start)

    @pl.when(origin_dev)
    def _():
        each_piece(lambda cp: cp.start())

        @pl.when(plane == y)
        def _():
            lo = pl.multiple_of(my_lo, 16)
            m_ref[pl.ds(pl.multiple_of(p * B + my_lo, 16), 16), tile(q)] = a_ref[0, pl.ds(lo, 16), :]
    pl.when(p < NP)(scatter_start)
    relay_tile(0)
    ring_tile(0)
    for t in range(1, 10):
        relay_tile(t)
    S[...] = jnp.zeros_like(S)
    start_b_event()
    half_tile(0)
    for t in range(1, 10):
        ring_tile(t)
    start_event()
    bx_event()

    row = lax.broadcasted_iota(jnp.int32, (B, B), 0)
    col = lax.broadcasted_iota(jnp.int32, (B, B), 1)

    def step(k, _):
        for t, (kk, kc, _) in enumerate(tiles):
            if kk == kc:
                pl.when(k == kk)(functools.partial(half_got, t))

        T[...] = S[tile(k), tile(k)] + m_ref[tile(k), tile(k)]

        def between(jb):
            for kk in range(NP):
                for ev in events.get((kk, jb), ()):
                    pl.when(k == kk)(ev)

        factor_tile(T, between)
        S[tile(k), tile(k)] = T[...]
        X = jnp.where(row >= col, T[...], 0.0)
        for t, (kk, kc, _) in enumerate(tiles):
            if kk != kc:
                pl.when(k == kk)(functools.partial(half_got, t))

        def solve(m, _):
            S[tile(k), tile(m)] = dot3(X, S[tile(k), tile(m)] + m_ref[tile(k), tile(m)])
            return 0

        lax.fori_loop(k + 1, NP, solve, 0)

        def trail(i, _):
            left = S[tile(k), tile(i)].T

            def inner(m, _):
                S[tile(i), tile(m)] = S[tile(i), tile(m)] - dot3(left, S[tile(k), tile(m)])
                return 0

            lax.fori_loop(i, NP, inner, 0)
            return 0

        lax.fori_loop(k + 1, NP, trail, 0)
        return 0

    lax.fori_loop(0, NP, step, 0)

    for i in range(2):
        for c in range(2):
            relay(1 - par + 2 * i, c).wait_recv()

    def block(i, j):
        return S[i * B:(i + 1) * B, j * B:(j + 1) * B]

    for k in range(NP):
        acc = g_ref[k * B:(k + 1) * B, :]
        for i in range(k):
            acc = acc - dot3(block(i, k).T, W[i * B:(i + 1) * B, :])
        W[k * B:(k + 1) * B, :] = dot3(jnp.where(row >= col, block(k, k), 0.0), acc)

    kq = jnp.minimum(q, NP - 1)
    kp = jnp.minimum(p, NP - 1)
    u = S[tile(kq), tile(kp)]
    u_diag = jnp.where(col > row, u, jnp.where(col == row, 1.0 / u, 0.0))
    u = jnp.where(kp == kq, u_diag, jnp.where(kq < kp, u, 0.0))
    l_ref[...] = u.T

    col2 = lax.broadcasted_iota(jnp.int32, (B, 2 * B), 1)
    row2 = lax.broadcasted_iota(jnp.int32, (B, 2 * B), 0)
    for k in (3, 2, 1, 0):
        unit = jnp.where((row2 == col2) & (q == k), 1.0, 0.0)
        acc = jnp.where((col2 < B) & (q < NP), unit, W[k * B:(k + 1) * B, :])
        for m in range(k + 1, NP):
            acc = acc - dot3(S[k * B:(k + 1) * B, m * B:(m + 1) * B], W[m * B:(m + 1) * B, :])
        X = jnp.where(row >= col, S[k * B:(k + 1) * B, k * B:(k + 1) * B], 0.0)
        w = dot3(X.T, acc)
        W[k * B:(k + 1) * B, :] = w
        hi, lo = split(w)
        whi_ref[k * B:(k + 1) * B, :] = hi
        wlo_ref[k * B:(k + 1) * B, :] = lo

    bz_event(4)
    for dz in range(8):
        ax2_event(dz)

    @pl.when(p < NP)
    def _():
        for c in range(2):
            for cp in origin(c):
                cp.wait_send()
            for b in (1, 0):
                pl.when(jnp.logical_not(scatter_self(c)))(scatter(c, b).wait_send)
    for c in range(2):
        for i in range(2):
            k = par + 2 * i
            pl.when(k != p)(relay(k, c).wait_send)
            cond, cp = onward(i, c)
            pl.when(cond)(cp.wait_send)
    pl.when(origin_dev)(lambda: each_piece(lambda cp: cp.wait_send()))
    for t in range(10):
        @pl.when((x == 0) & (y == tiles[t][2]))
        def _():
            for cp in relay_sends(t):
                cp.wait_send()

        def drain():
            for d in range(1, 8):
                ring_send(t, d).wait_send()
            if t:
                for cp in plane_sends(t):
                    cp.wait_send()
        when(in_plane(t), drain)
        half_send(t, par).wait_send()
    for n in range(3):
        bx(n).wait_send()
    for way in (1, -1):
        for n in range(last(way)):
            az(n, way).wait_send()
            bz(n, way).wait_send()
        for dz in range(8):
            ax(dz, way).wait_send()
            axf(dz, way).wait_send()


def main(a):
    dma = pltpu.SemaphoreType.DMA
    vmem = pl.BlockSpec(memory_space=pltpu.VMEM)
    return pl.pallas_call(
        main_kernel,
        out_shape=(
            jax.ShapeDtypeStruct((8, 4, B, B), F32),
            jax.ShapeDtypeStruct((TOP, 2 * B), BF16),
            jax.ShapeDtypeStruct((TOP, 2 * B), BF16),
            jax.ShapeDtypeStruct((B, B), F32),
        ),
        in_specs=[vmem],
        out_specs=[vmem] * 4,
        scratch_shapes=[
            pltpu.VMEM((2, B, B), F32),
            pltpu.VMEM((TOP, TOP), F32),
            pltpu.VMEM((TOP, 2 * B), F32),
            pltpu.VMEM((TOP, TOP), F32),
            pltpu.VMEM((B, B), F32),
            pltpu.VMEM((TOP, 2 * B), F32),
            dma((NP, 2)), dma((2, 3)), dma((NP, 2)), dma((2, 2)),
            dma((10,)), dma((10,)), dma((10, 8)), dma((10,)), dma((10,)),
            dma((2, 8)), dma((16,)), dma((10, 3)), dma((10, 8)), dma((10,)), dma((10, 3)),
            dma((2,)), dma((2, 2)), dma((8, 4)), dma((8, 2)), dma((8,)), dma((4,)),
            dma((7,)), dma((8, 4)), dma((3,)), dma((7,)),
        ],
        compiler_params=pltpu.CompilerParams(
            collective_id=1, has_side_effects=True, vmem_limit_bytes=30 * 1024 * 1024),
        cost_estimate=pl.CostEstimate(
            flops=60_000_000_000, bytes_accessed=8_000_000, transcendentals=0),
        name="main",
    )(a)


RG = 4


def update_kernel(p_ref, b_ref, m_ref, whi_ref, wlo_ref, l_ref, o_ref):
    first = pl.program_id(0) * RG
    p = p_ref[0]
    q = p_ref[1]

    def row_tile(r):
        return jnp.concatenate(
            [b_ref[(p + 4 * (r // 4) + k) % 8, r % 4].astype(BF16) for k in range(NP)], axis=1)

    left = jnp.concatenate([row_tile(first + n) for n in range(RG)], axis=0)
    acc = dot1(left, whi_ref[...]) + dot1(left, wlo_ref[...])
    factor_col = q < NP
    for n in range(RG):
        top = (first + n == 0) & (p < NP)
        m = m_ref[pl.ds(pl.multiple_of((first + n) * B, B), B)].astype(F32)
        a0 = acc[n * B:(n + 1) * B, 0:B]
        a1 = acc[n * B:(n + 1) * B, B:]
        c0 = jnp.where(factor_col, a0, m[:, 0, :] - a0)
        c0 = jnp.where(top, jnp.where(factor_col, l_ref[...], 0.0), c0)
        c1 = jnp.where(top, 0.0, m[:, 1, :] - a1)
        for h, part in enumerate((c0[:, :128], c0[:, 128:], c1[:, :128], c1[:, 128:])):
            o_ref[pl.ds(4 * B * n + h, B, stride=4), :] = part


def update(place, bulk, mine, whi, wlo, ltile):
    vmem = pl.BlockSpec(memory_space=pltpu.VMEM)
    return pl.pallas_call(
        update_kernel,
        out_shape=jax.ShapeDtypeStruct((8 * 4 * B, 128), F32),
        grid_spec=pltpu.PrefetchScalarGridSpec(
            num_scalar_prefetch=1,
            grid=(8 // RG,),
            in_specs=[vmem] * 5,
            out_specs=pl.BlockSpec((4 * B * RG, 128), lambda r, place: (r, 0)),
        ),
        compiler_params=pltpu.CompilerParams(vmem_limit_bytes=24 * 1024 * 1024),
        cost_estimate=pl.CostEstimate(
            flops=4_300_000_000, bytes_accessed=16_000_000, transcendentals=0),
        name="update",
    )(place, bulk, mine, whi, wlo, ltile)


def local(covariance):
    mine = covariance.reshape(8, B, 2, B)
    a = mine[0].astype(F32).transpose(1, 0, 2)
    mine = mine.reshape(8 * B, 2, B)
    bulk, whi, wlo, ltile = main(a)
    place = jnp.stack([lax.axis_index("prow"), lax.axis_index("pcol")]).astype(jnp.int32)
    out = update(place, bulk, mine, whi, wlo, ltile)
    return out.reshape(8, 1, B, 2, 1, B)


def solution(mesh):
    in_specs = (P(None, "prow", None, None, "pcol", None),)
    out_specs = P(None, "prow", None, None, "pcol", None)
    return jax.shard_map(local, mesh=mesh, in_specs=in_specs, out_specs=out_specs, check_vma=False)
```
